32 devices in a mesh: node: 4 (over z), local: 8 (over y, x, core).
Axes of the slice: x: 2, y: 2, z: 4, core: 2. Of those that a mesh axis runs over, the one named last changes fastest.
Arguments:
- acts: bfloat16 [2048, 8192], P('local', 'node'), may hold values from -6 to 6
- w_rot: bfloat16 [8192, 8192], P('local', 'node'), may hold values from -0.75 to 0.75
- signs: int32 [8192], replicated, may hold values from -1 to 1, as said below
- upstream: bfloat16 [2048, 8192], P('local', 'node'), may hold values from -6 to 6
Outputs:
- outputs: bfloat16 [2048, 8192], P('local', 'node')
- input_grad: bfloat16 [2048, 8192], P('local', 'node')
- grad_rot: float32 [8192, 8192], P('local', 'node')
The draws below stay inside these ranges and needn't reach their ends.
Inputs may be any that keep to these rules, and one draw needn't show every extreme that they name: `signs`: each entry is -1 or +1.
All inputs are finite; a program needn't handle non-finite values.
Results may differ from the reference program's by a relative error of at most 0.017.
Values may be sent and summed in bfloat16 or wider, within the bound.
A program may use at most 192 MiB of HBM per device.

```python
import jax
import jax.numpy as jnp
from jax import lax

D = 8192
HBLK = 128
TOK_DEV = 256
TOKENS = 2048
N_NODE = 4
N_LOCAL = 8


def draw_signs(key, part):
    return 2 * jax.random.randint(key, (D,), 0, 2, dtype=jnp.int32) - 1


def steps_of(key, dims, pieces, low, top_value):
    level, own = 1.0, jax.random.fold_in(key, 6)
    for dim, parts in pieces:
        steps = jnp.exp(jax.random.uniform(jax.random.fold_in(own, dim), (parts,), jnp.float32, low / len(pieces), top_value / len(pieces)))
        level = level * jnp.repeat(steps, dims[dim] // parts).reshape([-1 if axis == dim else 1 for axis in range(len(dims))])
    return level


def noise(stream_key, dims, scale, limit, split=(), kind=jnp.bfloat16):
    values = jax.random.normal(stream_key, dims, jnp.float32) * scale
    if len(split) > 0:
        values = steps_of(stream_key, dims, split, -0.22, 0.18) * values
    return jnp.clip(values, min=-limit, max=limit).astype(kind)


def setup_inputs(seed: int = 0) -> dict:
    key_list = jax.random.split(jax.random.key(seed), 5)
    return {
        "acts": noise(key_list[0], (TOKENS, D), 1.0, 6.0, ((0, 8), (1, 4))),
        "w_rot": noise(key_list[1], (D, D), ((HBLK / D) ** 0.5), 0.75, ((0, 8), (1, 4))),
        "signs": draw_signs(jax.random.fold_in(key_list[4], 71), 0),
        "upstream": noise(key_list[3], (TOKENS, D), 1.0, 6.0, ((0, 8), (1, 4))),
    }


def sylvester(order_count):
    row_index = lax.broadcasted_iota(jnp.int32, (order_count, order_count), 0)
    col_index = lax.broadcasted_iota(jnp.int32, (order_count, order_count), 1)
    common = jnp.bitwise_and(row_index, col_index)
    parity = jnp.zeros((order_count, order_count), jnp.int32)
    for bit_index in range(order_count.bit_length() - 1):
        parity = parity + jnp.bitwise_and(jnp.right_shift(common, bit_index), 1)
    return (1 - 2 * jnp.bitwise_and(parity, 1)).astype(jnp.float32)


def reference(acts, w_rot, signs, upstream):
    hadamard = sylvester(HBLK)
    sign_values = signs.astype(jnp.float32)
    blocks = w_rot.astype(jnp.float32).reshape(D // HBLK, HBLK, D)
    mixed = jnp.einsum("ij,bjc->bic", hadamard, blocks)
    weight = (mixed * (sign_values.reshape(D // HBLK, HBLK, 1) / HBLK)).reshape(D, D).astype(jnp.bfloat16)
    outputs = jnp.dot(acts, weight, preferred_element_type=jnp.float32).astype(jnp.bfloat16)
    col_group = D // N_NODE
    input_total = jnp.zeros((TOKENS, D), jnp.float32)
    for group_index in range(N_NODE):
        upper = upstream[:, group_index * col_group:(group_index + 1) * col_group]
        columns = weight[:, group_index * col_group:(group_index + 1) * col_group]
        term_value = jnp.dot(upper, columns.T, preferred_element_type=jnp.float32).astype(jnp.bfloat16)
        term_value = lax.optimization_barrier(term_value)
        input_total = input_total + term_value.astype(jnp.float32)
    input_grad = input_total.astype(jnp.bfloat16)
    signed = acts.astype(jnp.float32) * sign_values[None, :]
    rot_blocks = jnp.einsum("tbj,jk->tbk", signed.reshape(TOKENS, D // HBLK, HBLK), hadamard)
    acts_rot = (rot_blocks / HBLK).reshape(TOKENS, D).astype(jnp.bfloat16)
    grad_rot = jnp.zeros((D, D), jnp.float32)
    for group_index in range(N_LOCAL):
        rot_rows = acts_rot[group_index * TOK_DEV:(group_index + 1) * TOK_DEV]
        up_rows = upstream[group_index * TOK_DEV:(group_index + 1) * TOK_DEV]
        term_value = jnp.dot(rot_rows.T, up_rows, preferred_element_type=jnp.float32).astype(jnp.bfloat16)
        term_value = lax.optimization_barrier(term_value)
        grad_rot = grad_rot + term_value.astype(jnp.float32)
    return outputs, input_grad, grad_rot
```

```python
import jax
import jax.numpy as jnp
from jax import lax
from jax.sharding import PartitionSpec as P

HBLK = 128


def sylvester(order_count):
    row_index = lax.broadcasted_iota(jnp.int32, (order_count, order_count), 0)
    col_index = lax.broadcasted_iota(jnp.int32, (order_count, order_count), 1)
    common = jnp.bitwise_and(row_index, col_index)
    parity = jnp.zeros((order_count, order_count), jnp.int32)
    for bit_index in range(order_count.bit_length() - 1):
        parity = parity + jnp.bitwise_and(jnp.right_shift(common, bit_index), 1)
    return (1 - 2 * jnp.bitwise_and(parity, 1)).astype(jnp.float32)


def local(acts, w_rot, signs, upstream):
    rows, cols = w_rot.shape
    blocks = rows // HBLK
    had = sylvester(HBLK)
    own_signs = lax.dynamic_slice_in_dim(signs, lax.axis_index("local") * rows, rows)
    own_signs = own_signs.astype(jnp.float32).reshape(blocks, HBLK)
    up_all = lax.all_gather(upstream, "local", axis=0, tiled=True)
    feats = lax.all_gather(acts, "node", axis=1, tiled=True)
    own = lax.all_to_all(feats, "local", split_axis=1, concat_axis=0, tiled=True)

    left = (own_signs[:, :, None] * had).astype(jnp.bfloat16)
    mixed = jnp.einsum(
        "bij,bjc->bic", left, w_rot.reshape(blocks, HBLK, cols), preferred_element_type=jnp.float32
    )
    weight = (mixed / HBLK).astype(jnp.bfloat16).reshape(rows, cols)

    terms = lax.dot_general(
        up_all, weight, (((1,), (1,)), ((), ())), preferred_element_type=jnp.float32
    ).astype(jnp.bfloat16)
    terms = lax.all_to_all(terms, "local", split_axis=0, concat_axis=1, tiled=True)
    input_grad = lax.psum_scatter(terms, "node", scatter_dimension=1, tiled=True)

    partial = jnp.dot(own, weight, preferred_element_type=jnp.float32).astype(jnp.bfloat16)
    outputs = lax.psum_scatter(partial, "local", scatter_dimension=0, tiled=True)

    right = (own_signs[:, :, None] * had).astype(jnp.bfloat16)
    rotated = jnp.einsum(
        "tbj,bjk->tbk", own.reshape(-1, blocks, HBLK), right, preferred_element_type=jnp.float32
    )
    rotated = (rotated / HBLK).astype(jnp.bfloat16).reshape(-1, rows)
    grad_rot = lax.dot_general(
        rotated, up_all, (((0,), (0,)), ((), ())), preferred_element_type=jnp.float32
    )
    return outputs, input_grad, grad_rot


def solution(mesh):
    spec = P("local", "node")
    return jax.shard_map(
        local, mesh=mesh, in_specs=(spec, spec, P(), spec), out_specs=(spec, spec, spec), check_vma=False
    )
```

```python
import functools

import jax
import jax.numpy as jnp
from jax import lax
from jax.experimental import pallas as pl
from jax.experimental.pallas import tpu as pltpu
from jax.sharding import PartitionSpec as P

HBLK = 128


def sylvester(order_count):
    row_index = lax.broadcasted_iota(jnp.int32, (order_count, order_count), 0)
    col_index = lax.broadcasted_iota(jnp.int32, (order_count, order_count), 1)
    common = jnp.bitwise_and(row_index, col_index)
    parity = jnp.zeros((order_count, order_count), jnp.int32)
    for bit_index in range(order_count.bit_length() - 1):
        parity = parity + jnp.bitwise_and(jnp.right_shift(common, bit_index), 1)
    return (1 - 2 * jnp.bitwise_and(parity, 1)).astype(jnp.float32)


def local(acts, w_rot, signs, upstream):
    rows, cols = w_rot.shape
    blocks = rows // HBLK
    had = sylvester(HBLK)
    own_signs = lax.dynamic_slice_in_dim(signs, lax.axis_index("local") * rows, rows)
    own_signs = own_signs.astype(jnp.float32).reshape(blocks, HBLK)
    up_all = lax.all_gather(upstream, "local", axis=0, tiled=True)
    feats = lax.all_gather(acts, "node", axis=1, tiled=True)
    own = lax.all_to_all(feats, "local", split_axis=1, concat_axis=0, tiled=True)

    left = (own_signs[:, :, None] * had).astype(jnp.bfloat16)
    mixed = jnp.einsum(
        "bij,bjc->bic", left, w_rot.reshape(blocks, HBLK, cols), preferred_element_type=jnp.float32
    )
    weight = (mixed / HBLK).astype(jnp.bfloat16).reshape(rows, cols)

    terms = lax.dot_general(
        up_all, weight, (((1,), (1,)), ((), ())), preferred_element_type=jnp.float32
    ).astype(jnp.bfloat16)
    terms = lax.all_to_all(terms, "local", split_axis=0, concat_axis=1, tiled=True)
    input_grad = lax.psum_scatter(terms, "node", scatter_dimension=1, tiled=True)

    partial = jnp.dot(own, weight, preferred_element_type=jnp.float32).astype(jnp.bfloat16)
    outputs = lax.psum_scatter(partial, "local", scatter_dimension=0, tiled=True)

    right = (own_signs[:, :, None] * had).astype(jnp.bfloat16)
    rotated = jnp.einsum(
        "tbj,bjk->tbk", own.reshape(-1, blocks, HBLK), right, preferred_element_type=jnp.float32
    )
    rotated = (rotated / HBLK).astype(jnp.bfloat16).reshape(-1, rows)
    grad_rot = lax.dot_general(
        rotated, up_all, (((0,), (0,)), ((), ())), preferred_element_type=jnp.float32
    )
    return outputs, input_grad, grad_rot


SUB = 4
TILE = 512
GRAD_TILE = 256
MESH = pl.DeviceIdType.MESH


def kernel(n, acts_ref, wrot_ref, up_ref, left_ref, right_ref,
           out_ref, ig_ref, grad_ref,
           w_raw, w, x, xo, rot, u, pi, below, above, po, rs_long, rs_short, gt,
           load_sem, d1_send, d1_recv, x_send, x_recv, xo_send, xo_recv,
           e_long, e_short, e_sib, u_recv, w_sem, c_send, c_recv, f_send, f_recv,
           rl_send, rl_recv, rr_send, rr_recv, g_sem):
    half = n // 2
    tok, feats = acts_ref.shape
    rows, cols = wrot_ref.shape
    sub_tok = tok // SUB
    pieces = n * SUB
    l = lax.axis_index("local")
    z = lax.axis_index("node")
    p, c = lax.div(l, 2), lax.rem(l, 2)
    s = 1 - 2 * c
    column, line = lax.rem(p, 2), lax.div(p, 2)
    r = column * (n - 1 - line) + (1 - column) * line

    def ring(offset):
        at = lax.rem(r + offset + 2 * n, n)
        far = lax.div(at, half)
        return (1 - far) * (2 * at) + far * (2 * (n - 1 - at) + 1)

    ge = lax.div(z - p + n, n)
    le = lax.div(p - z + n, n)
    home = ge * le
    dist = (1 - le) * (z - p) + (1 - ge) * (p - z)
    upper = lax.div(2 * p, n)
    c_lag = (1 - ge) * z + (1 - le) * (n - 1 - z) + home * (
        upper * p + (1 - upper) * (n - 1 - p))
    goes_up = jnp.logical_and(z >= p, z < n - 1)
    goes_down = jnp.logical_and(z <= p, z > 0)
    from_below = goes_down
    from_above = goes_up

    def dev(chip, core, node):
        return {"local": 2 * chip + core, "node": node}

    sibling = dev(p, 1 - c, z)
    long_nb, short_nb = dev(ring(s), c, z), dev(ring(-s), c, z)

    def remote(src, dst, send, recv, to):
        return pltpu.make_async_remote_copy(
            src_ref=src, dst_ref=dst, send_sem=send, recv_sem=recv,
            device_id=to, device_id_type=MESH)

    def u_rows(index):
        return pl.ds(pl.multiple_of(index * tok, tok), tok)

    def part(index):
        return pl.ds(pl.multiple_of(index * sub_tok, sub_tok), sub_tok)

    barrier = pltpu.get_barrier_semaphore()
    for k in range(1, n):
        pl.semaphore_signal(barrier, inc=1, device_id=dev(ring(k), c, z), device_id_type=MESH)
    pl.semaphore_signal(barrier, inc=1, device_id=sibling, device_id_type=MESH)

    @pl.when(z > 0)
    def _():
        pl.semaphore_signal(barrier, inc=1, device_id=dev(p, c, z - 1), device_id_type=MESH)

    @pl.when(z < n - 1)
    def _():
        pl.semaphore_signal(barrier, inc=1, device_id=dev(p, c, z + 1), device_id_type=MESH)

    load_w = pltpu.make_async_copy(wrot_ref, w_raw, load_sem.at[0])
    load_w.start()
    load_u = pltpu.make_async_copy(up_ref, u.at[u_rows(l)], load_sem.at[1])
    load_u.start()
    load_x = pltpu.make_async_copy(acts_ref, x.at[p], load_sem.at[2])

    @pl.when(home == 1)
    def _():
        load_x.start()

    pl.semaphore_wait(barrier, n + 2 - lax.div(n - z, n) - lax.div(z + 1, n))

    d1 = remote(acts_ref, x.at[p], d1_send, d1_recv.at[p], dev(z, c, z))

    @pl.when(home == 0)
    def _():
        d1.start()

    load_u.wait()

    def e_copy_long(step):
        at = u_rows(2 * ring(-s * (step - 1)) + c)
        return remote(u.at[at], u.at[at], e_long.at[step - 1],
                      u_recv.at[2 * ring(-s * (step - 1)) + c], long_nb)

    def e_copy_short(step):
        at = u_rows(2 * ring(s * (step - 1)) + c)
        return remote(u.at[at], u.at[at], e_short.at[step - 1],
                      u_recv.at[2 * ring(s * (step - 1)) + c], short_nb)

    def e_copy_sib(chip):
        at = u_rows(2 * chip + c)
        return remote(u.at[at], u.at[at], e_sib.at[chip], u_recv.at[2 * chip + c], sibling)

    def u_arrived(index):
        pltpu.make_async_copy(u.at[u_rows(index)], u.at[u_rows(index)], u_recv.at[index]).wait()

    e_copy_long(1).start()
    e_copy_short(1).start()

    load_w.wait()
    own_rows = pl.ds(pl.multiple_of(c * rows, rows), rows)

    @pl.loop(0, rows // HBLK)
    def _(b):
        at = pl.ds(pl.multiple_of(b * HBLK, HBLK), HBLK)
        to = pl.ds(pl.multiple_of(c * rows + b * HBLK, HBLK), HBLK)
        mixed = jnp.dot(left_ref[b], w_raw[at, :], preferred_element_type=jnp.float32)
        w[to, :] = (mixed * (1.0 / HBLK)).astype(jnp.bfloat16)

    w_copy = remote(w.at[own_rows], w.at[own_rows], w_sem.at[0], w_sem.at[1], sibling)
    w_copy.start()
    e_copy_sib(p).start()

    def x_chip(i):
        moved = lax.div(i + n - 1, n) * (half - lax.div(i, 2)) * (1 - 2 * lax.rem(i, 2))
        return ring(moved * s)

    def c_chip(i):
        return ring(lax.div(i + 1, 2) * (1 - 2 * lax.rem(i, 2)) * s)

    def x_copy(q, sub, way, node):
        at = part(sub)
        return remote(x.at[q, at], x.at[q, at], x_send.at[way, q * SUB + sub],
                      x_recv.at[q * SUB + sub], dev(p, c, node))

    def xo_copy(q):
        cut = pl.ds(pl.multiple_of((1 - c) * rows, rows), rows)
        return remote(x.at[q, :, cut], xo.at[q], xo_send.at[q], xo_recv.at[q], sibling)

    def c_copy_up(q, sub):
        return remote(pi.at[q, part(sub)], below.at[q, part(sub)], c_send.at[q * SUB + sub],
                      c_recv.at[0, q * SUB + sub], dev(p, c, z + 1))

    def c_copy_down(q, sub):
        return remote(pi.at[q, part(sub)], above.at[q, part(sub)], c_send.at[q * SUB + sub],
                      c_recv.at[1, q * SUB + sub], dev(p, c, z - 1))

    def f_copy(q, sub):
        return remote(pi.at[q, part(sub)], ig_ref.at[part(sub)], f_send.at[q * SUB + sub],
                      f_recv.at[sub], dev(q, c, z))

    def rl_copy(k):
        return remote(po.at[ring(s * k)], rs_long.at[k - 1], rl_send.at[k - 1],
                      rl_recv.at[k - 1], long_nb)

    def rr_copy(k):
        return remote(po.at[ring(-s * k)], rs_short.at[k - 1], rr_send.at[k - 1],
                      rr_recv.at[k - 1], short_nb)

    def rotate(q, index, read):
        at = pl.ds(pl.multiple_of(index * tok, tok), tok)
        for b in range(rows // HBLK):
            turned = lax.dot_general(right_ref[b], read(b), (((1,), (1,)), ((), ())),
                                     preferred_element_type=jnp.float32)
            rot[b * HBLK:(b + 1) * HBLK, at] = (turned * (1.0 / HBLK)).astype(jnp.bfloat16)

    def add_into(total, piece):
        return (total.astype(jnp.float32) + piece.astype(jnp.float32)).astype(jnp.bfloat16)

    c_start = 2
    slots = c_start + n - 1 + pieces

    @pl.loop(0, slots)
    def _(t):
        @pl.when(t == c_start)
        def _():
            w_copy.wait_recv()

        for step in range(1, half + 1):
            @pl.when(t == SUB * step)
            def _(step=step):
                first = ring(-s * step)
                u_arrived(2 * first + c)
                if step < half:
                    e_copy_long(step + 1).start()
                e_copy_sib(first).start()
                if step < half:
                    second = ring(s * step)
                    u_arrived(2 * second + c)
                    if step < half - 1:
                        e_copy_short(step + 1).start()
                    e_copy_sib(second).start()

        j = t - dist

        @pl.when(jnp.logical_and(j >= 0, j < pieces))
        def _():
            i, sub = lax.div(j, SUB), lax.rem(j, SUB)
            q = x_chip(i)

            @pl.when(jnp.logical_and(home == 1, j == 0))
            def _():
                load_x.wait()

            @pl.when(jnp.logical_and(home == 1, jnp.logical_and(sub == 0, j > 0)))
            def _():
                pltpu.make_async_copy(x.at[q], x.at[q], d1_recv.at[q]).wait()

            @pl.when(home == 0)
            def _():
                pltpu.make_async_copy(x.at[q, part(sub)], x.at[q, part(sub)],
                                      x_recv.at[q * SUB + sub]).wait()

            @pl.when(goes_up)
            def _():
                x_copy(q, sub, 0, z + 1).start()

            @pl.when(goes_down)
            def _():
                x_copy(q, sub, 1, z - 1).start()

            @pl.when(sub == SUB - 1)
            def _():
                xo_copy(q).start()

                @pl.loop(0, cols // TILE)
                def _(tile):
                    at = pl.ds(pl.multiple_of(tile * TILE, TILE), TILE)
                    po[q, :, at] = jnp.dot(
                        x[q], w[:, at], preferred_element_type=jnp.float32).astype(jnp.bfloat16)

                rotate(q, 2 * q + c, lambda b: x[
                    q, :, pl.ds(pl.multiple_of(c * rows + b * HBLK, HBLK), HBLK)])

        jc = t - c_start - c_lag

        @pl.when(jnp.logical_and(jc >= 0, jc < pieces))
        def _():
            i, sub = lax.div(jc, SUB), lax.rem(jc, SUB)
            q = c_chip(i)
            at = part(sub)

            @pl.when(sub == 0)
            def _():
                @pl.loop(0, feats // TILE)
                def _(tile):
                    cut = pl.ds(pl.multiple_of(tile * TILE, TILE), TILE)
                    pi[q, :, cut] = lax.dot_general(
                        u[u_rows(2 * q + c), :], w[cut, :], (((1,), (1,)), ((), ())),
                        preferred_element_type=jnp.float32).astype(jnp.bfloat16)

            @pl.when(from_below)
            def _():
                pltpu.make_async_copy(below.at[q, at], below.at[q, at],
                                      c_recv.at[0, q * SUB + sub]).wait()
                pi[q, at, :] = add_into(pi[q, at, :], below[q, at, :])

            @pl.when(from_above)
            def _():
                pltpu.make_async_copy(above.at[q, at], above.at[q, at],
                                      c_recv.at[1, q * SUB + sub]).wait()
                pi[q, at, :] = add_into(pi[q, at, :], above[q, at, :])

            @pl.when(z < p)
            def _():
                c_copy_up(q, sub).start()

            @pl.when(z > p)
            def _():
                c_copy_down(q, sub).start()

            @pl.when(jnp.logical_and(home == 1, q == p))
            def _():
                ig_ref[at, :] = pi[q, at, :]

            @pl.when(jnp.logical_and(home == 1, q != p))
            def _():
                f_copy(q, sub).start()

        for k in range(half, 0, -1):
            i = 1 if k == half else 2 * (half - k)

            @pl.when(t == n - 1 + SUB * i + SUB - 1)
            def _(k=k):
                if k < half:
                    rl_copy(k + 1).wait_recv()
                    q = ring(s * k)
                    po[q] = add_into(po[q], rs_long[k])
                rl_copy(k).start()

        for k in range(half - 1, 0, -1):
            @pl.when(t == n - 1 + SUB * (2 * (half - k) + 1) + SUB - 1)
            def _(k=k):
                if k < half - 1:
                    rr_copy(k + 1).wait_recv()
                    q = ring(-s * k)
                    po[q] = add_into(po[q], rs_short[k])
                rr_copy(k).start()

    @pl.loop(0, n)
    def _(q):
        pltpu.make_async_copy(xo.at[q], xo.at[q], xo_recv.at[q]).wait()
        u_arrived(2 * q + 1 - c)
        rotate(q, 2 * q + 1 - c, lambda b: xo[q, :, b * HBLK:(b + 1) * HBLK])

    def g_copy(tile, slot):
        at = pl.ds(pl.multiple_of(tile * GRAD_TILE, GRAD_TILE), GRAD_TILE)
        return pltpu.make_async_copy(gt.at[slot], grad_ref.at[:, at], g_sem.at[slot])

    tiles = cols // GRAD_TILE

    @pl.loop(0, tiles)
    def _(tile):
        slot = lax.rem(tile, 2)

        @pl.when(tile >= 2)
        def _():
            g_copy(tile - 2, slot).wait()

        at = pl.ds(pl.multiple_of(tile * GRAD_TILE, GRAD_TILE), GRAD_TILE)
        gt[slot] = jnp.dot(rot[...], u[:, at], preferred_element_type=jnp.float32)
        g_copy(tile, slot).start()

    rl_copy(1).wait_recv()
    rr_copy(1).wait_recv()
    out_ref[...] = (po[p].astype(jnp.float32) + rs_long[0].astype(jnp.float32)
                    + rs_short[0].astype(jnp.float32)).astype(jnp.bfloat16)

    @pl.when(home == 0)
    def _():
        for sub in range(SUB):
            pltpu.make_async_copy(ig_ref.at[part(sub)], ig_ref.at[part(sub)], f_recv.at[sub]).wait()
        d1.wait_send()

    for tile in (tiles - 2, tiles - 1):
        g_copy(tile, tile % 2).wait()
    w_copy.wait_send()
    for step in range(1, half + 1):
        e_copy_long(step).wait_send()
        rl_copy(step).wait_send()
    for step in range(1, half):
        e_copy_short(step).wait_send()
        rr_copy(step).wait_send()

    @pl.loop(0, n)
    def _(q):
        e_copy_sib(q).wait_send()
        xo_copy(q).wait_send()

        @pl.loop(0, SUB)
        def _(sub):
            @pl.when(goes_up)
            def _():
                x_copy(q, sub, 0, z + 1).wait_send()

            @pl.when(goes_down)
            def _():
                x_copy(q, sub, 1, z - 1).wait_send()

            @pl.when(z < p)
            def _():
                c_copy_up(q, sub).wait_send()

            @pl.when(z > p)
            def _():
                c_copy_down(q, sub).wait_send()

            @pl.when(jnp.logical_and(home == 1, q != p))
            def _():
                f_copy(q, sub).wait_send()


def fused(acts, w_rot, signs, upstream):
    n = lax.axis_size("node")
    tok, feats = acts.shape
    rows, cols = w_rot.shape
    blocks = rows // HBLK
    half = n // 2
    had = sylvester(HBLK)
    own_signs = lax.dynamic_slice_in_dim(signs, lax.axis_index("local") * rows, rows)
    own_signs = own_signs.astype(jnp.float32).reshape(blocks, HBLK)
    left = (own_signs[:, :, None] * had).astype(jnp.bfloat16)
    right = (own_signs[:, None, :] * had).astype(jnp.bfloat16)
    bf = jnp.bfloat16
    dma = pltpu.SemaphoreType.DMA
    vmem = pl.BlockSpec(memory_space=pltpu.VMEM)
    hbm = pl.BlockSpec(memory_space=pl.ANY)
    tokens = 2 * n * tok
    return pl.pallas_call(
        functools.partial(kernel, n),
        out_shape=(
            jax.ShapeDtypeStruct((tok, cols), bf),
            jax.ShapeDtypeStruct((tok, feats), bf),
            jax.ShapeDtypeStruct((rows, cols), jnp.float32),
        ),
        in_specs=[hbm, hbm, hbm, vmem, vmem],
        out_specs=(vmem, vmem, hbm),
        scratch_shapes=[
            pltpu.VMEM((rows, cols), bf),
            pltpu.VMEM((feats, cols), bf),
            pltpu.VMEM((n, tok, feats), bf),
            pltpu.VMEM((n, tok, rows), bf),
            pltpu.VMEM((rows, tokens), bf),
            pltpu.VMEM((tokens, cols), bf),
            pltpu.VMEM((n, tok, feats), bf),
            pltpu.VMEM((n, tok, feats), bf),
            pltpu.VMEM((n, tok, feats), bf),
            pltpu.VMEM((n, tok, cols), bf),
            pltpu.VMEM((half, tok, cols), bf),
            pltpu.VMEM((half - 1, tok, cols), bf),
            pltpu.VMEM((2, rows, GRAD_TILE), jnp.float32),
            dma((3,)), dma, dma((n,)), dma((2, n * SUB)), dma((n * SUB,)), dma((n,)), dma((n,)),
            dma((half,)), dma((half - 1,)), dma((n,)), dma((2 * n,)), dma((2,)),
            dma((n * SUB,)), dma((2, n * SUB)), dma((n * SUB,)), dma((SUB,)),
            dma((half,)), dma((half,)), dma((half - 1,)), dma((half - 1,)), dma((2,)),
        ],
        compiler_params=pltpu.CompilerParams(
            collective_id=0, has_side_effects=True, vmem_limit_bytes=60 << 20),
        cost_estimate=pl.CostEstimate(
            flops=6 * tokens * rows * cols, bytes_accessed=16 * rows * cols, transcendentals=0),
    )(acts, w_rot, upstream, left, right)


def solution(mesh):
    spec = P("local", "node")
    n = mesh.shape["node"]
    paired = mesh.shape["local"] == 2 * n and n >= 4 and n % 2 == 0
    return jax.shard_map(
        fused if paired else local, mesh=mesh, in_specs=(spec, spec, P(), spec),
        out_specs=(spec, spec, spec), check_vma=False,
    )
```

```python
import functools

import jax
import jax.numpy as jnp
from jax import lax
from jax.experimental import pallas as pl
from jax.experimental.pallas import tpu as pltpu
from jax.sharding import PartitionSpec as P

HBLK = 128


def sylvester(order_count):
    row_index = lax.broadcasted_iota(jnp.int32, (order_count, order_count), 0)
    col_index = lax.broadcasted_iota(jnp.int32, (order_count, order_count), 1)
    common = jnp.bitwise_and(row_index, col_index)
    parity = jnp.zeros((order_count, order_count), jnp.int32)
    for bit_index in range(order_count.bit_length() - 1):
        parity = parity + jnp.bitwise_and(jnp.right_shift(common, bit_index), 1)
    return (1 - 2 * jnp.bitwise_and(parity, 1)).astype(jnp.float32)


def local(acts, w_rot, signs, upstream):
    rows, cols = w_rot.shape
    blocks = rows // HBLK
    had = sylvester(HBLK)
    own_signs = lax.dynamic_slice_in_dim(signs, lax.axis_index("local") * rows, rows)
    own_signs = own_signs.astype(jnp.float32).reshape(blocks, HBLK)
    up_all = lax.all_gather(upstream, "local", axis=0, tiled=True)
    feats = lax.all_gather(acts, "node", axis=1, tiled=True)
    own = lax.all_to_all(feats, "local", split_axis=1, concat_axis=0, tiled=True)

    left = (own_signs[:, :, None] * had).astype(jnp.bfloat16)
    mixed = jnp.einsum(
        "bij,bjc->bic", left, w_rot.reshape(blocks, HBLK, cols), preferred_element_type=jnp.float32
    )
    weight = (mixed / HBLK).astype(jnp.bfloat16).reshape(rows, cols)

    terms = lax.dot_general(
        up_all, weight, (((1,), (1,)), ((), ())), preferred_element_type=jnp.float32
    ).astype(jnp.bfloat16)
    terms = lax.all_to_all(terms, "local", split_axis=0, concat_axis=1, tiled=True)
    input_grad = lax.psum_scatter(terms, "node", scatter_dimension=1, tiled=True)

    partial = jnp.dot(own, weight, preferred_element_type=jnp.float32).astype(jnp.bfloat16)
    outputs = lax.psum_scatter(partial, "local", scatter_dimension=0, tiled=True)

    right = (own_signs[:, :, None] * had).astype(jnp.bfloat16)
    rotated = jnp.einsum(
        "tbj,bjk->tbk", own.reshape(-1, blocks, HBLK), right, preferred_element_type=jnp.float32
    )
    rotated = (rotated / HBLK).astype(jnp.bfloat16).reshape(-1, rows)
    grad_rot = lax.dot_general(
        rotated, up_all, (((0,), (0,)), ((), ())), preferred_element_type=jnp.float32
    )
    return outputs, input_grad, grad_rot


SUB = 4
TILE = 512
GRAD_TILE = 256
MESH = pl.DeviceIdType.MESH


def kernel(n, acts_ref, wrot_ref, up_ref, left_ref, right_ref,
           out_ref, ig_ref, grad_ref,
           w_raw, w, x, xo, rot, u, pi, below, above, po, rs_long, rs_short, gt,
           load_sem, d1_send, d1_recv, x_send, x_recv, xo_send, xo_recv,
           e_long, e_short, e_sib, u_recv, w_sem, c_send, c_recv, f_send, f_recv,
           rl_send, rl_recv, rr_send, rr_recv, g_sem):
    half = n // 2
    tok, feats = acts_ref.shape
    rows, cols = wrot_ref.shape
    sub_tok = tok // SUB
    pieces = n * SUB
    l = lax.axis_index("local")
    z = lax.axis_index("node")
    p, c = lax.div(l, 2), lax.rem(l, 2)
    s = 1 - 2 * c
    column, line = lax.rem(p, 2), lax.div(p, 2)
    r = column * (n - 1 - line) + (1 - column) * line

    def ring(offset):
        at = lax.rem(r + offset + 2 * n, n)
        far = lax.div(at, half)
        return (1 - far) * (2 * at) + far * (2 * (n - 1 - at) + 1)

    ge = lax.div(z - p + n, n)
    le = lax.div(p - z + n, n)
    home = ge * le
    dist = (1 - le) * (z - p) + (1 - ge) * (p - z)
    upper = lax.div(2 * p, n)
    c_lag = (1 - ge) * z + (1 - le) * (n - 1 - z) + home * (
        upper * p + (1 - upper) * (n - 1 - p))
    goes_up = jnp.logical_and(z >= p, z < n - 1)
    goes_down = jnp.logical_and(z <= p, z > 0)
    from_below = goes_down
    from_above = goes_up

    def dev(chip, core, node):
        return {"local": 2 * chip + core, "node": node}

    sibling = dev(p, 1 - c, z)
    long_nb, short_nb = dev(ring(s), c, z), dev(ring(-s), c, z)

    def remote(src, dst, send, recv, to):
        return pltpu.make_async_remote_copy(
            src_ref=src, dst_ref=dst, send_sem=send, recv_sem=recv,
            device_id=to, device_id_type=MESH)

    def u_rows(index):
        return pl.ds(pl.multiple_of(index * tok, tok), tok)

    def part(index):
        return pl.ds(pl.multiple_of(index * sub_tok, sub_tok), sub_tok)

    barrier = pltpu.get_barrier_semaphore()
    for k in range(1, n):
        pl.semaphore_signal(barrier, inc=1, device_id=dev(ring(k), c, z), device_id_type=MESH)
    pl.semaphore_signal(barrier, inc=1, device_id=sibling, device_id_type=MESH)

    @pl.when(z > 0)
    def _():
        pl.semaphore_signal(barrier, inc=1, device_id=dev(p, c, z - 1), device_id_type=MESH)

    @pl.when(z < n - 1)
    def _():
        pl.semaphore_signal(barrier, inc=1, device_id=dev(p, c, z + 1), device_id_type=MESH)

    load_w = pltpu.make_async_copy(wrot_ref, w_raw, load_sem.at[0])
    load_w.start()
    load_u = pltpu.make_async_copy(up_ref, u.at[u_rows(l)], load_sem.at[1])
    load_u.start()
    load_x = pltpu.make_async_copy(acts_ref, x.at[p], load_sem.at[2])

    @pl.when(home == 1)
    def _():
        load_x.start()

    pl.semaphore_wait(barrier, n + 2 - lax.div(n - z, n) - lax.div(z + 1, n))

    d1 = remote(acts_ref, x.at[p], d1_send, d1_recv.at[p], dev(z, c, z))

    home_column, home_line = lax.rem(z, 2), lax.div(z, 2)
    home_r = home_column * (n - 1 - home_line) + (1 - home_column) * home_line
    away = lax.rem(s * (r - home_r) + 2 * n, n)
    past = lax.div(away + half - 1, n)
    arc = past * (n - away) + (1 - past) * away
    turn = 2 * (half - arc) + past + lax.div(arc, half)

    @pl.when(jnp.logical_and(home == 0, turn == 1))
    def _():
        d1.start()

    load_u.wait()

    def e_copy_long(step):
        at = u_rows(2 * ring(-s * (step - 1)) + c)
        return remote(u.at[at], u.at[at], e_long.at[step - 1],
                      u_recv.at[2 * ring(-s * (step - 1)) + c], long_nb)

    def e_copy_short(step):
        at = u_rows(2 * ring(s * (step - 1)) + c)
        return remote(u.at[at], u.at[at], e_short.at[step - 1],
                      u_recv.at[2 * ring(s * (step - 1)) + c], short_nb)

    def e_copy_sib(chip):
        at = u_rows(2 * chip + c)
        return remote(u.at[at], u.at[at], e_sib.at[chip], u_recv.at[2 * chip + c], sibling)

    def u_arrived(index):
        pltpu.make_async_copy(u.at[u_rows(index)], u.at[u_rows(index)], u_recv.at[index]).wait()

    e_copy_long(1).start()
    own_rows = pl.ds(pl.multiple_of(c * rows, rows), rows)
    w_copy = remote(w.at[own_rows], w.at[own_rows], w_sem.at[0], w_sem.at[1], sibling)

    def x_chip(i):
        moved = lax.div(i + n - 1, n) * (half - lax.div(i, 2)) * (1 - 2 * lax.rem(i, 2))
        return ring(moved * s)

    def c_chip(i):
        return ring(lax.div(i + 1, 2) * (1 - 2 * lax.rem(i, 2)) * s)

    def x_copy(q, sub, way, node):
        at = part(sub)
        return remote(x.at[q, at], x.at[q, at], x_send.at[way, q * SUB + sub],
                      x_recv.at[q * SUB + sub], dev(p, c, node))

    def xo_copy(q):
        cut = pl.ds(pl.multiple_of((1 - c) * rows, rows), rows)
        return remote(x.at[q, :, cut], xo.at[q], xo_send.at[q], xo_recv.at[q], sibling)

    def c_copy_up(q, sub):
        return remote(pi.at[q, part(sub)], below.at[q, part(sub)], c_send.at[q * SUB + sub],
                      c_recv.at[0, q * SUB + sub], dev(p, c, z + 1))

    def c_copy_down(q, sub):
        return remote(pi.at[q, part(sub)], above.at[q, part(sub)], c_send.at[q * SUB + sub],
                      c_recv.at[1, q * SUB + sub], dev(p, c, z - 1))

    def f_copy(q, sub):
        return remote(pi.at[q, part(sub)], ig_ref.at[part(sub)], f_send.at[q * SUB + sub],
                      f_recv.at[sub], dev(q, c, z))

    def rl_copy(k):
        return remote(po.at[ring(s * k)], rs_long.at[k - 1], rl_send.at[k - 1],
                      rl_recv.at[k - 1], long_nb)

    def rr_copy(k):
        return remote(po.at[ring(-s * k)], rs_short.at[k - 1], rr_send.at[k - 1],
                      rr_recv.at[k - 1], short_nb)

    def rotate(q, index, read):
        at = pl.ds(pl.multiple_of(index * tok, tok), tok)
        for b in range(rows // HBLK):
            turned = lax.dot_general(right_ref[b], read(b), (((1,), (1,)), ((), ())),
                                     preferred_element_type=jnp.float32)
            rot[b * HBLK:(b + 1) * HBLK, at] = (turned * (1.0 / HBLK)).astype(jnp.bfloat16)

    def rotate_own(q):
        rotate(q, 2 * q + c, lambda b: x[
            q, :, pl.ds(pl.multiple_of(c * rows + b * HBLK, HBLK), HBLK)])

    def out_tile(q, tile):
        at = pl.ds(pl.multiple_of(tile * tile_cols, tile_cols), tile_cols)
        po[q, :, at] = jnp.dot(
            x[q], w[:, at], preferred_element_type=jnp.float32).astype(jnp.bfloat16)

    def add_into(total, piece):
        return (total.astype(jnp.float32) + piece.astype(jnp.float32)).astype(jnp.bfloat16)

    c_start = 3
    tile_cols = cols // SUB
    slots = c_start + n - 1 + pieces

    @pl.loop(0, slots)
    def _(t):
        @pl.when(t == c_start)
        def _():
            w_copy.wait_recv()

        @pl.when(jnp.logical_and(t == SUB * turn - 5, jnp.logical_and(home == 0, turn > 1)))
        def _():
            d1.start()

        @pl.when(t == 2)
        def _():
            e_copy_short(1).start()

        for step in range(1, half + 1):
            @pl.when(t == SUB * (2 * step - 1) + 1)
            def _(step=step):
                source = ring(-s * step)
                u_arrived(2 * source + c)
                if step < half:
                    e_copy_long(step + 1).start()
                e_copy_sib(source).start()

        for step in range(1, half):
            @pl.when(t == 2 * SUB * step + 1)
            def _(step=step):
                source = ring(s * step)
                u_arrived(2 * source + c)
                if step < half - 1:
                    e_copy_short(step + 1).start()
                e_copy_sib(source).start()

        j = t - dist

        @pl.when(jnp.logical_and(j >= 0, j < pieces))
        def _():
            i, sub = lax.div(j, SUB), lax.rem(j, SUB)
            q = x_chip(i)

            @pl.when(jnp.logical_and(home == 1, j == 0))
            def _():
                load_x.wait()

            @pl.when(jnp.logical_and(home == 1, jnp.logical_and(sub == 0, j > 0)))
            def _():
                pltpu.make_async_copy(x.at[q], x.at[q], d1_recv.at[q]).wait()

            @pl.when(home == 0)
            def _():
                pltpu.make_async_copy(x.at[q, part(sub)], x.at[q, part(sub)],
                                      x_recv.at[q * SUB + sub]).wait()

            @pl.when(goes_up)
            def _():
                x_copy(q, sub, 0, z + 1).start()

            @pl.when(goes_down)
            def _():
                x_copy(q, sub, 1, z - 1).start()

            @pl.when(sub == SUB - 1)
            def _():
                xo_copy(q).start()

            @pl.when(jnp.logical_and(i > 0, sub < 2))
            def _():
                done = x_chip(i - 1)
                for tile in range(SUB // 2):
                    out_tile(done, sub * (SUB // 2) + tile)

            @pl.when(jnp.logical_and(i > 0, sub == 2))
            def _():
                rotate_own(x_chip(i - 1))

            @pl.when(j == pieces - 1)
            def _():
                @pl.loop(0, SUB)
                def _(tile):
                    out_tile(q, tile)

        @pl.when(t == 0)
        def _():
            load_w.wait()

            @pl.loop(0, rows // HBLK)
            def _(b):
                at = pl.ds(pl.multiple_of(b * HBLK, HBLK), HBLK)
                to = pl.ds(pl.multiple_of(c * rows + b * HBLK, HBLK), HBLK)
                mixed = jnp.dot(left_ref[b], w_raw[at, :], preferred_element_type=jnp.float32)
                w[to, :] = (mixed * (1.0 / HBLK)).astype(jnp.bfloat16)

            w_copy.start()
            e_copy_sib(p).start()

        jc = t - c_start - c_lag

        @pl.when(jnp.logical_and(jc >= 0, jc < pieces))
        def _():
            i, sub = lax.div(jc, SUB), lax.rem(jc, SUB)
            q = c_chip(i)
            at = part(sub)

            @pl.when(sub == 0)
            def _():
                @pl.loop(0, feats // TILE)
                def _(tile):
                    cut = pl.ds(pl.multiple_of(tile * TILE, TILE), TILE)
                    pi[q, :, cut] = lax.dot_general(
                        u[u_rows(2 * q + c), :], w[cut, :], (((1,), (1,)), ((), ())),
                        preferred_element_type=jnp.float32).astype(jnp.bfloat16)

            @pl.when(from_below)
            def _():
                pltpu.make_async_copy(below.at[q, at], below.at[q, at],
                                      c_recv.at[0, q * SUB + sub]).wait()
                pi[q, at, :] = add_into(pi[q, at, :], below[q, at, :])

            @pl.when(from_above)
            def _():
                pltpu.make_async_copy(above.at[q, at], above.at[q, at],
                                      c_recv.at[1, q * SUB + sub]).wait()
                pi[q, at, :] = add_into(pi[q, at, :], above[q, at, :])

            @pl.when(z < p)
            def _():
                c_copy_up(q, sub).start()

            @pl.when(z > p)
            def _():
                c_copy_down(q, sub).start()

            @pl.when(jnp.logical_and(home == 1, q == p))
            def _():
                ig_ref[at, :] = pi[q, at, :]

            @pl.when(jnp.logical_and(home == 1, q != p))
            def _():
                f_copy(q, sub).start()

        for k in range(half, 0, -1):
            i = 1 if k == half else 2 * (half - k)

            @pl.when(t == n - 1 + SUB * i + SUB + 1)
            def _(k=k):
                if k < half:
                    rl_copy(k + 1).wait_recv()
                    q = ring(s * k)
                    po[q] = add_into(po[q], rs_long[k])
                rl_copy(k).start()

        for k in range(half - 1, 0, -1):
            @pl.when(t == n - 1 + SUB * (2 * (half - k) + 1) + SUB - 1 + 2 * min(k - 1, 1))
            def _(k=k):
                if k < half - 1:
                    rr_copy(k + 1).wait_recv()
                    q = ring(-s * k)
                    po[q] = add_into(po[q], rs_short[k])
                rr_copy(k).start()

    rotate_own(x_chip(n - 1))

    @pl.loop(0, n)
    def _(q):
        pltpu.make_async_copy(xo.at[q], xo.at[q], xo_recv.at[q]).wait()
        u_arrived(2 * q + 1 - c)
        rotate(q, 2 * q + 1 - c, lambda b: xo[q, :, b * HBLK:(b + 1) * HBLK])

    def g_copy(tile, slot):
        at = pl.ds(pl.multiple_of(tile * GRAD_TILE, GRAD_TILE), GRAD_TILE)
        return pltpu.make_async_copy(gt.at[slot], grad_ref.at[:, at], g_sem.at[slot])

    tiles = cols // GRAD_TILE

    @pl.loop(0, tiles)
    def _(tile):
        slot = lax.rem(tile, 2)

        @pl.when(tile >= 2)
        def _():
            g_copy(tile - 2, slot).wait()

        at = pl.ds(pl.multiple_of(tile * GRAD_TILE, GRAD_TILE), GRAD_TILE)
        gt[slot] = jnp.dot(rot[...], u[:, at], preferred_element_type=jnp.float32)
        g_copy(tile, slot).start()

    rl_copy(1).wait_recv()
    rr_copy(1).wait_recv()
    out_ref[...] = (po[p].astype(jnp.float32) + rs_long[0].astype(jnp.float32)
                    + rs_short[0].astype(jnp.float32)).astype(jnp.bfloat16)

    @pl.when(home == 0)
    def _():
        for sub in range(SUB):
            pltpu.make_async_copy(ig_ref.at[part(sub)], ig_ref.at[part(sub)], f_recv.at[sub]).wait()
        d1.wait_send()

    for tile in (tiles - 2, tiles - 1):
        g_copy(tile, tile % 2).wait()
    w_copy.wait_send()
    for step in range(1, half + 1):
        e_copy_long(step).wait_send()
        rl_copy(step).wait_send()
    for step in range(1, half):
        e_copy_short(step).wait_send()
        rr_copy(step).wait_send()

    @pl.loop(0, n)
    def _(q):
        e_copy_sib(q).wait_send()
        xo_copy(q).wait_send()

        @pl.loop(0, SUB)
        def _(sub):
            @pl.when(goes_up)
            def _():
                x_copy(q, sub, 0, z + 1).wait_send()

            @pl.when(goes_down)
            def _():
                x_copy(q, sub, 1, z - 1).wait_send()

            @pl.when(z < p)
            def _():
                c_copy_up(q, sub).wait_send()

            @pl.when(z > p)
            def _():
                c_copy_down(q, sub).wait_send()

            @pl.when(jnp.logical_and(home == 1, q != p))
            def _():
                f_copy(q, sub).wait_send()


COPY_PARTS = 8


def copy_kernel(out_ref, ig_ref, grad_ref, out_to, ig_to, grad_to, sems):
    copies = [pltpu.make_async_copy(out_ref, out_to, sems.at[0]),
              pltpu.make_async_copy(ig_ref, ig_to, sems.at[1])]
    rows = grad_ref.shape[0] // COPY_PARTS
    for part in range(COPY_PARTS):
        at = pl.ds(part * rows, rows)
        copies.append(pltpu.make_async_copy(grad_ref.at[at], grad_to.at[at], sems.at[2 + part]))
    for copy in copies:
        copy.start()
    for copy in copies:
        copy.wait()


def hand_on(arrays):
    hbm = pl.BlockSpec(memory_space=pl.ANY)
    return pl.pallas_call(
        copy_kernel,
        out_shape=tuple(jax.ShapeDtypeStruct(a.shape, a.dtype) for a in arrays),
        in_specs=[hbm] * 3,
        out_specs=(hbm,) * 3,
        scratch_shapes=[pltpu.SemaphoreType.DMA((2 + COPY_PARTS,))],
    )(*arrays)


def fused(acts, w_rot, signs, upstream):
    n = lax.axis_size("node")
    tok, feats = acts.shape
    rows, cols = w_rot.shape
    blocks = rows // HBLK
    half = n // 2
    had = sylvester(HBLK)
    own_signs = lax.dynamic_slice_in_dim(signs, lax.axis_index("local") * rows, rows)
    own_signs = own_signs.astype(jnp.float32).reshape(blocks, HBLK)
    left = (own_signs[:, :, None] * had).astype(jnp.bfloat16)
    right = (own_signs[:, None, :] * had).astype(jnp.bfloat16)
    bf = jnp.bfloat16
    dma = pltpu.SemaphoreType.DMA
    vmem = pl.BlockSpec(memory_space=pltpu.VMEM)
    hbm = pl.BlockSpec(memory_space=pl.ANY)
    tokens = 2 * n * tok
    return hand_on(pl.pallas_call(
        functools.partial(kernel, n),
        out_shape=(
            jax.ShapeDtypeStruct((tok, cols), bf),
            jax.ShapeDtypeStruct((tok, feats), bf),
            jax.ShapeDtypeStruct((rows, cols), jnp.float32),
        ),
        in_specs=[hbm, hbm, hbm, vmem, vmem],
        out_specs=(vmem, vmem, hbm),
        scratch_shapes=[
            pltpu.VMEM((rows, cols), bf),
            pltpu.VMEM((feats, cols), bf),
            pltpu.VMEM((n, tok, feats), bf),
            pltpu.VMEM((n, tok, rows), bf),
            pltpu.VMEM((rows, tokens), bf),
            pltpu.VMEM((tokens, cols), bf),
            pltpu.VMEM((n, tok, feats), bf),
            pltpu.VMEM((n, tok, feats), bf),
            pltpu.VMEM((n, tok, feats), bf),
            pltpu.VMEM((n, tok, cols), bf),
            pltpu.VMEM((half, tok, cols), bf),
            pltpu.VMEM((half - 1, tok, cols), bf),
            pltpu.VMEM((2, rows, GRAD_TILE), jnp.float32),
            dma((3,)), dma, dma((n,)), dma((2, n * SUB)), dma((n * SUB,)), dma((n,)), dma((n,)),
            dma((half,)), dma((half - 1,)), dma((n,)), dma((2 * n,)), dma((2,)),
            dma((n * SUB,)), dma((2, n * SUB)), dma((n * SUB,)), dma((SUB,)),
            dma((half,)), dma((half,)), dma((half - 1,)), dma((half - 1,)), dma((2,)),
        ],
        compiler_params=pltpu.CompilerParams(
            collective_id=0, has_side_effects=True, vmem_limit_bytes=60 << 20),
        cost_estimate=pl.CostEstimate(
            flops=6 * tokens * rows * cols, bytes_accessed=16 * rows * cols, transcendentals=0),
    )(acts, w_rot, upstream, left, right))


def solution(mesh):
    spec = P("local", "node")
    n = mesh.shape["node"]
    paired = mesh.shape["local"] == 2 * n and n >= 4 and n % 2 == 0
    return jax.shard_map(
        fused if paired else local, mesh=mesh, in_specs=(spec, spec, P(), spec),
        out_specs=(spec, spec, spec), check_vma=False,
    )
```

```python
import functools

import jax
import jax.numpy as jnp
from jax import lax
from jax.experimental import pallas as pl
from jax.experimental.pallas import tpu as pltpu
from jax.sharding import PartitionSpec as P

HBLK = 128


def sylvester(order_count):
    row_index = lax.broadcasted_iota(jnp.int32, (order_count, order_count), 0)
    col_index = lax.broadcasted_iota(jnp.int32, (order_count, order_count), 1)
    common = jnp.bitwise_and(row_index, col_index)
    parity = jnp.zeros((order_count, order_count), jnp.int32)
    for bit_index in range(order_count.bit_length() - 1):
        parity = parity + jnp.bitwise_and(jnp.right_shift(common, bit_index), 1)
    return (1 - 2 * jnp.bitwise_and(parity, 1)).astype(jnp.float32)


def local(acts, w_rot, signs, upstream):
    rows, cols = w_rot.shape
    blocks = rows // HBLK
    had = sylvester(HBLK)
    own_signs = lax.dynamic_slice_in_dim(signs, lax.axis_index("local") * rows, rows)
    own_signs = own_signs.astype(jnp.float32).reshape(blocks, HBLK)
    up_all = lax.all_gather(upstream, "local", axis=0, tiled=True)
    feats = lax.all_gather(acts, "node", axis=1, tiled=True)
    own = lax.all_to_all(feats, "local", split_axis=1, concat_axis=0, tiled=True)

    left = (own_signs[:, :, None] * had).astype(jnp.bfloat16)
    mixed = jnp.einsum(
        "bij,bjc->bic", left, w_rot.reshape(blocks, HBLK, cols), preferred_element_type=jnp.float32
    )
    weight = (mixed / HBLK).astype(jnp.bfloat16).reshape(rows, cols)

    terms = lax.dot_general(
        up_all, weight, (((1,), (1,)), ((), ())), preferred_element_type=jnp.float32
    ).astype(jnp.bfloat16)
    terms = lax.all_to_all(terms, "local", split_axis=0, concat_axis=1, tiled=True)
    input_grad = lax.psum_scatter(terms, "node", scatter_dimension=1, tiled=True)

    partial = jnp.dot(own, weight, preferred_element_type=jnp.float32).astype(jnp.bfloat16)
    outputs = lax.psum_scatter(partial, "local", scatter_dimension=0, tiled=True)

    right = (own_signs[:, :, None] * had).astype(jnp.bfloat16)
    rotated = jnp.einsum(
        "tbj,bjk->tbk", own.reshape(-1, blocks, HBLK), right, preferred_element_type=jnp.float32
    )
    rotated = (rotated / HBLK).astype(jnp.bfloat16).reshape(-1, rows)
    grad_rot = lax.dot_general(
        rotated, up_all, (((0,), (0,)), ((), ())), preferred_element_type=jnp.float32
    )
    return outputs, input_grad, grad_rot


SUB = 8
TILES = 4
TILE = 512
GRAD_TILE = 256
MESH = pl.DeviceIdType.MESH


def swapped(n, i):
    one = lax.div(i + n - 1, n) - lax.div(i + n - 2, n)
    two = lax.div(i + n - 2, n) - lax.div(i + n - 3, n)
    return i + one - two


def kernel(n, acts_ref, wrot_ref, up_ref, left_ref, right_ref,
           out_ref, ig_ref, grad_ref,
           w_raw, w, x, xo, rot, u, pi, below, above, po, rs_long, rs_short, gt,
           load_sem, d1_send, d1_recv, x_send, x_recv, xo_send, xo_recv,
           e_long, e_short, e_sib, u_recv, w_sem, c_send, c_recv, f_send, f_recv,
           rl_send, rl_recv, rr_send, rr_recv, g_sem):
    half = n // 2
    tok, feats = acts_ref.shape
    rows, cols = wrot_ref.shape
    sub_tok = tok // SUB
    pieces = n * SUB
    l = lax.axis_index("local")
    z = lax.axis_index("node")
    p, c = lax.div(l, 2), lax.rem(l, 2)
    s = 1 - 2 * c
    column, line = lax.rem(p, 2), lax.div(p, 2)
    r = column * (n - 1 - line) + (1 - column) * line

    def ring(offset):
        at = lax.rem(r + offset + 2 * n, n)
        far = lax.div(at, half)
        return (1 - far) * (2 * at) + far * (2 * (n - 1 - at) + 1)

    ge = lax.div(z - p + n, n)
    le = lax.div(p - z + n, n)
    home = ge * le
    dist = (1 - le) * (z - p) + (1 - ge) * (p - z)
    upper = lax.div(2 * p, n)
    c_lag = (1 - ge) * z + (1 - le) * (n - 1 - z) + home * (
        upper * p + (1 - upper) * (n - 1 - p))
    goes_up = jnp.logical_and(z >= p, z < n - 1)
    goes_down = jnp.logical_and(z <= p, z > 0)
    from_below = goes_down
    from_above = goes_up

    def dev(chip, core, node):
        return {"local": 2 * chip + core, "node": node}

    sibling = dev(p, 1 - c, z)
    long_nb, short_nb = dev(ring(s), c, z), dev(ring(-s), c, z)

    def remote(src, dst, send, recv, to):
        return pltpu.make_async_remote_copy(
            src_ref=src, dst_ref=dst, send_sem=send, recv_sem=recv,
            device_id=to, device_id_type=MESH)

    def u_rows(index):
        return pl.ds(pl.multiple_of(index * tok, tok), tok)

    def part(index):
        return pl.ds(pl.multiple_of(index * sub_tok, sub_tok), sub_tok)

    barrier = pltpu.get_barrier_semaphore()
    for k in range(1, n):
        pl.semaphore_signal(barrier, inc=1, device_id=dev(ring(k), c, z), device_id_type=MESH)
    pl.semaphore_signal(barrier, inc=1, device_id=sibling, device_id_type=MESH)

    @pl.when(z > 0)
    def _():
        pl.semaphore_signal(barrier, inc=1, device_id=dev(p, c, z - 1), device_id_type=MESH)

    @pl.when(z < n - 1)
    def _():
        pl.semaphore_signal(barrier, inc=1, device_id=dev(p, c, z + 1), device_id_type=MESH)

    load_w = pltpu.make_async_copy(wrot_ref, w_raw, load_sem.at[0])
    load_w.start()
    load_u = pltpu.make_async_copy(up_ref, u.at[u_rows(l)], load_sem.at[1])
    load_u.start()
    load_x = pltpu.make_async_copy(acts_ref, x.at[p], load_sem.at[2])

    @pl.when(home == 1)
    def _():
        load_x.start()

    pl.semaphore_wait(barrier, n + 2 - lax.div(n - z, n) - lax.div(z + 1, n))

    d1 = remote(acts_ref, x.at[p], d1_send, d1_recv.at[p], dev(z, c, z))

    home_column, home_line = lax.rem(z, 2), lax.div(z, 2)
    home_r = home_column * (n - 1 - home_line) + (1 - home_column) * home_line
    away = lax.rem(s * (r - home_r) + 2 * n, n)
    past = lax.div(away + half - 1, n)
    arc = past * (n - away) + (1 - past) * away
    turn = swapped(n, 2 * (half - arc) + past + lax.div(arc, half))

    @pl.when(jnp.logical_and(home == 0, turn == 1))
    def _():
        d1.start()

    load_u.wait()

    def e_copy_long(step):
        at = u_rows(2 * ring(-s * (step - 1)) + c)
        return remote(u.at[at], u.at[at], e_long.at[step - 1],
                      u_recv.at[2 * ring(-s * (step - 1)) + c], long_nb)

    def e_copy_short(step):
        at = u_rows(2 * ring(s * (step - 1)) + c)
        return remote(u.at[at], u.at[at], e_short.at[step - 1],
                      u_recv.at[2 * ring(s * (step - 1)) + c], short_nb)

    def e_copy_sib(chip):
        at = u_rows(2 * chip + c)
        return remote(u.at[at], u.at[at], e_sib.at[chip], u_recv.at[2 * chip + c], sibling)

    def u_arrived(index):
        pltpu.make_async_copy(u.at[u_rows(index)], u.at[u_rows(index)], u_recv.at[index]).wait()

    own_rows = pl.ds(pl.multiple_of(c * rows, rows), rows)
    w_copy = remote(w.at[own_rows], w.at[own_rows], w_sem.at[0], w_sem.at[1], sibling)

    def x_chip(i):
        i = swapped(n, i)
        moved = lax.div(i + n - 1, n) * (half - lax.div(i, 2)) * (1 - 2 * lax.rem(i, 2))
        return ring(moved * s)

    def c_chip(i):
        return ring(lax.div(i + 1, 2) * (1 - 2 * lax.rem(i, 2)) * s)

    def x_copy(q, sub, way, node):
        at = part(sub)
        return remote(x.at[q, at], x.at[q, at], x_send.at[way, q * SUB + sub],
                      x_recv.at[q * SUB + sub], dev(p, c, node))

    def xo_copy(q):
        cut = pl.ds(pl.multiple_of((1 - c) * rows, rows), rows)
        return remote(x.at[q, :, cut], xo.at[q], xo_send.at[q], xo_recv.at[q], sibling)

    def c_copy_up(q, sub):
        return remote(pi.at[q, part(sub)], below.at[q, part(sub)], c_send.at[q * SUB + sub],
                      c_recv.at[0, q * SUB + sub], dev(p, c, z + 1))

    def c_copy_down(q, sub):
        return remote(pi.at[q, part(sub)], above.at[q, part(sub)], c_send.at[q * SUB + sub],
                      c_recv.at[1, q * SUB + sub], dev(p, c, z - 1))

    def f_copy(q, sub):
        return remote(pi.at[q, part(sub)], ig_ref.at[part(sub)], f_send.at[q * SUB + sub],
                      f_recv.at[sub], dev(q, c, z))

    def rl_copy(k):
        return remote(po.at[ring(s * k)], rs_long.at[k - 1], rl_send.at[k - 1],
                      rl_recv.at[k - 1], long_nb)

    def rr_copy(k):
        return remote(po.at[ring(-s * k)], rs_short.at[k - 1], rr_send.at[k - 1],
                      rr_recv.at[k - 1], short_nb)

    def rotate(q, index, read):
        at = pl.ds(pl.multiple_of(index * tok, tok), tok)
        for b in range(rows // HBLK):
            turned = lax.dot_general(right_ref[b], read(b), (((1,), (1,)), ((), ())),
                                     preferred_element_type=jnp.float32)
            rot[b * HBLK:(b + 1) * HBLK, at] = (turned * (1.0 / HBLK)).astype(jnp.bfloat16)

    def rotate_own(q):
        rotate(q, 2 * q + c, lambda b: x[
            q, :, pl.ds(pl.multiple_of(c * rows + b * HBLK, HBLK), HBLK)])

    def out_tile(q, tile):
        at = pl.ds(pl.multiple_of(tile * tile_cols, tile_cols), tile_cols)
        po[q, :, at] = jnp.dot(
            x[q], w[:, at], preferred_element_type=jnp.float32).astype(jnp.bfloat16)

    def add_into(total, piece):
        return (total.astype(jnp.float32) + piece.astype(jnp.float32)).astype(jnp.bfloat16)

    c_start = 4
    tile_cols = cols // TILES
    slots = c_start + n - 1 + pieces

    @pl.loop(0, slots)
    def _(t):
        @pl.when(t == c_start)
        def _():
            w_copy.wait_recv()

        @pl.when(jnp.logical_and(t == SUB * turn - SUB // 2 - 10, jnp.logical_and(home == 0, turn > 1)))
        def _():
            d1.start()

        @pl.when(t == 3)
        def _():
            e_copy_long(1).start()

        @pl.when(t == 8)
        def _():
            e_copy_short(1).start()

        for step in range(1, half + 1):
            @pl.when(t == SUB * (2 * step - 1))
            def _(step=step):
                source = ring(-s * step)
                u_arrived(2 * source + c)
                if step < half:
                    e_copy_long(step + 1).start()
                e_copy_sib(source).start()

        for step in range(1, half):
            @pl.when(t == 2 * SUB * step)
            def _(step=step):
                source = ring(s * step)
                u_arrived(2 * source + c)
                if step < half - 1:
                    e_copy_short(step + 1).start()
                e_copy_sib(source).start()

        j = t - dist

        @pl.when(jnp.logical_and(j >= 0, j < pieces))
        def _():
            turns, sub = lax.div(j + SUB // 2, SUB), lax.rem(j + SUB // 2, SUB)
            q = x_chip(lax.rem(turns, n))

            @pl.when(jnp.logical_and(home == 1, j == 0))
            def _():
                load_x.wait()

            @pl.when(jnp.logical_and(
                home == 1, jnp.logical_and(sub == 0, turns < n)))
            def _():
                pltpu.make_async_copy(x.at[q], x.at[q], d1_recv.at[q]).wait()

            @pl.when(home == 0)
            def _():
                pltpu.make_async_copy(x.at[q, part(sub)], x.at[q, part(sub)],
                                      x_recv.at[q * SUB + sub]).wait()

            @pl.when(goes_up)
            def _():
                x_copy(q, sub, 0, z + 1).start()

            @pl.when(goes_down)
            def _():
                x_copy(q, sub, 1, z - 1).start()

            @pl.when(jnp.logical_or(j == pieces - 1, jnp.logical_and(sub == SUB - 1, turns > 0)))
            def _():
                xo_copy(q).start()

            @pl.when(jnp.logical_and(turns > 1, sub < 2))
            def _():
                done = x_chip(turns - 1)
                for tile in range(TILES // 2):
                    out_tile(done, sub * (TILES // 2) + tile)

            @pl.when(jnp.logical_and(turns > 1, sub == 3))
            def _():
                rotate_own(x_chip(turns - 1))

        @pl.when(t == 0)
        def _():
            load_w.wait()

            @pl.loop(0, rows // HBLK)
            def _(b):
                at = pl.ds(pl.multiple_of(b * HBLK, HBLK), HBLK)
                to = pl.ds(pl.multiple_of(c * rows + b * HBLK, HBLK), HBLK)
                mixed = jnp.dot(left_ref[b], w_raw[at, :], preferred_element_type=jnp.float32)
                w[to, :] = (mixed * (1.0 / HBLK)).astype(jnp.bfloat16)

            w_copy.start()
            e_copy_sib(p).start()

        jc = t - c_start - c_lag

        @pl.when(jnp.logical_and(jc >= 0, jc < pieces))
        def _():
            i, sub = lax.div(jc, SUB), lax.rem(jc, SUB)
            q = c_chip(i)
            at = part(sub)

            @pl.when(sub == 0)
            def _():
                @pl.loop(0, feats // TILE)
                def _(tile):
                    cut = pl.ds(pl.multiple_of(tile * TILE, TILE), TILE)
                    pi[q, :, cut] = lax.dot_general(
                        u[u_rows(2 * q + c), :], w[cut, :], (((1,), (1,)), ((), ())),
                        preferred_element_type=jnp.float32).astype(jnp.bfloat16)

            @pl.when(from_below)
            def _():
                pltpu.make_async_copy(below.at[q, at], below.at[q, at],
                                      c_recv.at[0, q * SUB + sub]).wait()
                pi[q, at, :] = add_into(pi[q, at, :], below[q, at, :])

            @pl.when(from_above)
            def _():
                pltpu.make_async_copy(above.at[q, at], above.at[q, at],
                                      c_recv.at[1, q * SUB + sub]).wait()
                pi[q, at, :] = add_into(pi[q, at, :], above[q, at, :])

            @pl.when(z < p)
            def _():
                c_copy_up(q, sub).start()

            @pl.when(z > p)
            def _():
                c_copy_down(q, sub).start()

            @pl.when(jnp.logical_and(home == 1, q == p))
            def _():
                ig_ref[at, :] = pi[q, at, :]

            @pl.when(jnp.logical_and(home == 1, q != p))
            def _():
                f_copy(q, sub).start()

        def rs_slot(i):
            return n - 1 + SUB * i + SUB // 2 + 1

        for k in range(half, 0, -1):
            at = rs_slot(2 if k == half else 2 * (half - k)) + (SUB // 2 + 1) * (k == half - 1)

            @pl.when(t == at)
            def _(k=k):
                if k < half:
                    rl_copy(k + 1).wait_recv()
                    q = ring(s * k)
                    po[q] = add_into(po[q], rs_long[k])
                rl_copy(k).start()

        for k in range(half - 1, 0, -1):
            @pl.when(t == rs_slot(2 * (half - k) + 1))
            def _(k=k):
                if k < half - 1:
                    rr_copy(k + 1).wait_recv()
                    q = ring(-s * k)
                    po[q] = add_into(po[q], rs_short[k])
                rr_copy(k).start()

    @pl.loop(0, TILES)
    def _(tile):
        out_tile(p, tile)

    rotate_own(p)

    @pl.loop(0, n)
    def _(q):
        pltpu.make_async_copy(xo.at[q], xo.at[q], xo_recv.at[q]).wait()
        u_arrived(2 * q + 1 - c)
        rotate(q, 2 * q + 1 - c, lambda b: xo[q, :, b * HBLK:(b + 1) * HBLK])

    def g_copy(tile, slot):
        at = pl.ds(pl.multiple_of(tile * GRAD_TILE, GRAD_TILE), GRAD_TILE)
        return pltpu.make_async_copy(gt.at[slot], grad_ref.at[:, at], g_sem.at[slot])

    tiles = cols // GRAD_TILE

    @pl.loop(0, tiles)
    def _(tile):
        slot = lax.rem(tile, 2)

        @pl.when(tile >= 2)
        def _():
            g_copy(tile - 2, slot).wait()

        at = pl.ds(pl.multiple_of(tile * GRAD_TILE, GRAD_TILE), GRAD_TILE)
        gt[slot] = jnp.dot(rot[...], u[:, at], preferred_element_type=jnp.float32)
        g_copy(tile, slot).start()

    rl_copy(1).wait_recv()
    rr_copy(1).wait_recv()
    out_ref[...] = (po[p].astype(jnp.float32) + rs_long[0].astype(jnp.float32)
                    + rs_short[0].astype(jnp.float32)).astype(jnp.bfloat16)

    @pl.when(home == 0)
    def _():
        for sub in range(SUB):
            pltpu.make_async_copy(ig_ref.at[part(sub)], ig_ref.at[part(sub)], f_recv.at[sub]).wait()
        d1.wait_send()

    for tile in (tiles - 2, tiles - 1):
        g_copy(tile, tile % 2).wait()
    w_copy.wait_send()
    for step in range(1, half + 1):
        e_copy_long(step).wait_send()
        rl_copy(step).wait_send()
    for step in range(1, half):
        e_copy_short(step).wait_send()
        rr_copy(step).wait_send()

    @pl.loop(0, n)
    def _(q):
        e_copy_sib(q).wait_send()
        xo_copy(q).wait_send()

        @pl.loop(0, SUB)
        def _(sub):
            @pl.when(goes_up)
            def _():
                x_copy(q, sub, 0, z + 1).wait_send()

            @pl.when(goes_down)
            def _():
                x_copy(q, sub, 1, z - 1).wait_send()

            @pl.when(z < p)
            def _():
                c_copy_up(q, sub).wait_send()

            @pl.when(z > p)
            def _():
                c_copy_down(q, sub).wait_send()

            @pl.when(jnp.logical_and(home == 1, q != p))
            def _():
                f_copy(q, sub).wait_send()


COPY_PARTS = 8


def copy_kernel(*refs):
    for source, target in zip(refs[:3], refs[3:]):
        target[...] = source[...]


def hand_on(arrays):
    specs = [pl.BlockSpec((a.shape[0] // COPY_PARTS, a.shape[1]), lambda i: (i, 0)) for a in arrays]
    return pl.pallas_call(
        copy_kernel,
        grid=(COPY_PARTS,),
        out_shape=tuple(jax.ShapeDtypeStruct(a.shape, a.dtype) for a in arrays),
        in_specs=specs,
        out_specs=tuple(specs),
        compiler_params=pltpu.CompilerParams(vmem_limit_bytes=32 << 20),
    )(*arrays)


def fused(acts, w_rot, signs, upstream):
    n = lax.axis_size("node")
    tok, feats = acts.shape
    rows, cols = w_rot.shape
    blocks = rows // HBLK
    half = n // 2
    had = sylvester(HBLK)
    own_signs = lax.dynamic_slice_in_dim(signs, lax.axis_index("local") * rows, rows)
    own_signs = own_signs.astype(jnp.float32).reshape(blocks, HBLK)
    left = (own_signs[:, :, None] * had).astype(jnp.bfloat16)
    right = (own_signs[:, None, :] * had).astype(jnp.bfloat16)
    bf = jnp.bfloat16
    dma = pltpu.SemaphoreType.DMA
    vmem = pl.BlockSpec(memory_space=pltpu.VMEM)
    hbm = pl.BlockSpec(memory_space=pl.ANY)
    tokens = 2 * n * tok
    return hand_on(pl.pallas_call(
        functools.partial(kernel, n),
        out_shape=(
            jax.ShapeDtypeStruct((tok, cols), bf),
            jax.ShapeDtypeStruct((tok, feats), bf),
            jax.ShapeDtypeStruct((rows, cols), jnp.float32),
        ),
        in_specs=[hbm, hbm, hbm, vmem, vmem],
        out_specs=(vmem, vmem, hbm),
        scratch_shapes=[
            pltpu.VMEM((rows, cols), bf),
            pltpu.VMEM((feats, cols), bf),
            pltpu.VMEM((n, tok, feats), bf),
            pltpu.VMEM((n, tok, rows), bf),
            pltpu.VMEM((rows, tokens), bf),
            pltpu.VMEM((tokens, cols), bf),
            pltpu.VMEM((n, tok, feats), bf),
            pltpu.VMEM((n, tok, feats), bf),
            pltpu.VMEM((n, tok, feats), bf),
            pltpu.VMEM((n, tok, cols), bf),
            pltpu.VMEM((half, tok, cols), bf),
            pltpu.VMEM((half - 1, tok, cols), bf),
            pltpu.VMEM((2, rows, GRAD_TILE), jnp.float32),
            dma((3,)), dma, dma((n,)), dma((2, n * SUB)), dma((n * SUB,)), dma((n,)), dma((n,)),
            dma((half,)), dma((half - 1,)), dma((n,)), dma((2 * n,)), dma((2,)),
            dma((n * SUB,)), dma((2, n * SUB)), dma((n * SUB,)), dma((SUB,)),
            dma((half,)), dma((half,)), dma((half - 1,)), dma((half - 1,)), dma((2,)),
        ],
        compiler_params=pltpu.CompilerParams(
            collective_id=0, has_side_effects=True, vmem_limit_bytes=60 << 20),
        cost_estimate=pl.CostEstimate(
            flops=6 * tokens * rows * cols, bytes_accessed=16 * rows * cols, transcendentals=0),
    )(acts, w_rot, upstream, left, right))


def solution(mesh):
    spec = P("local", "node")
    n = mesh.shape["node"]
    paired = mesh.shape["local"] == 2 * n and n >= 4 and n % 2 == 0
    return jax.shard_map(
        fused if paired else local, mesh=mesh, in_specs=(spec, spec, P(), spec),
        out_specs=(spec, spec, spec), check_vma=False,
    )
```

```python
import functools

import jax
import jax.numpy as jnp
from jax import lax
from jax.experimental import pallas as pl
from jax.experimental.pallas import tpu as pltpu
from jax.sharding import PartitionSpec as P

HBLK = 128


def sylvester(order_count):
    row_index = lax.broadcasted_iota(jnp.int32, (order_count, order_count), 0)
    col_index = lax.broadcasted_iota(jnp.int32, (order_count, order_count), 1)
    common = jnp.bitwise_and(row_index, col_index)
    parity = jnp.zeros((order_count, order_count), jnp.int32)
    for bit_index in range(order_count.bit_length() - 1):
        parity = parity + jnp.bitwise_and(jnp.right_shift(common, bit_index), 1)
    return (1 - 2 * jnp.bitwise_and(parity, 1)).astype(jnp.float32)


def local(acts, w_rot, signs, upstream):
    rows, cols = w_rot.shape
    blocks = rows // HBLK
    had = sylvester(HBLK)
    own_signs = lax.dynamic_slice_in_dim(signs, lax.axis_index("local") * rows, rows)
    own_signs = own_signs.astype(jnp.float32).reshape(blocks, HBLK)
    up_all = lax.all_gather(upstream, "local", axis=0, tiled=True)
    feats = lax.all_gather(acts, "node", axis=1, tiled=True)
    own = lax.all_to_all(feats, "local", split_axis=1, concat_axis=0, tiled=True)

    left = (own_signs[:, :, None] * had).astype(jnp.bfloat16)
    mixed = jnp.einsum(
        "bij,bjc->bic", left, w_rot.reshape(blocks, HBLK, cols), preferred_element_type=jnp.float32
    )
    weight = (mixed / HBLK).astype(jnp.bfloat16).reshape(rows, cols)

    terms = lax.dot_general(
        up_all, weight, (((1,), (1,)), ((), ())), preferred_element_type=jnp.float32
    ).astype(jnp.bfloat16)
    terms = lax.all_to_all(terms, "local", split_axis=0, concat_axis=1, tiled=True)
    input_grad = lax.psum_scatter(terms, "node", scatter_dimension=1, tiled=True)

    partial = jnp.dot(own, weight, preferred_element_type=jnp.float32).astype(jnp.bfloat16)
    outputs = lax.psum_scatter(partial, "local", scatter_dimension=0, tiled=True)

    right = (own_signs[:, :, None] * had).astype(jnp.bfloat16)
    rotated = jnp.einsum(
        "tbj,bjk->tbk", own.reshape(-1, blocks, HBLK), right, preferred_element_type=jnp.float32
    )
    rotated = (rotated / HBLK).astype(jnp.bfloat16).reshape(-1, rows)
    grad_rot = lax.dot_general(
        rotated, up_all, (((0,), (0,)), ((), ())), preferred_element_type=jnp.float32
    )
    return outputs, input_grad, grad_rot


SUB = 4
TILE = 512
GRAD_TILE = 256
MESH = pl.DeviceIdType.MESH


def kernel(n, acts_ref, wrot_ref, up_ref, left_ref, right_ref,
           out_ref, ig_ref, grad_ref,
           w_raw, w, x, xo, rot, u, pi, below, above, po, rs_long, rs_short, gt,
           load_sem, d1_send, d1_recv, x_send, x_recv, xo_send, xo_recv,
           e_long, e_short, e_sib, u_recv, w_sem, c_send, c_recv, f_send, f_recv,
           rl_send, rl_recv, rr_send, rr_recv, g_sem):
    half = n // 2
    tok, feats = acts_ref.shape
    rows, cols = wrot_ref.shape
    sub_tok = tok // SUB
    pieces = n * SUB
    l = lax.axis_index("local")
    z = lax.axis_index("node")
    p, c = lax.div(l, 2), lax.rem(l, 2)
    s = 1 - 2 * c
    column, line = lax.rem(p, 2), lax.div(p, 2)
    r = column * (n - 1 - line) + (1 - column) * line

    def ring(offset):
        at = lax.rem(r + offset + 2 * n, n)
        far = lax.div(at, half)
        return (1 - far) * (2 * at) + far * (2 * (n - 1 - at) + 1)

    ge = lax.div(z - p + n, n)
    le = lax.div(p - z + n, n)
    home = ge * le
    dist = (1 - le) * (z - p) + (1 - ge) * (p - z)
    upper = lax.div(2 * p, n)
    c_lag = (1 - ge) * z + (1 - le) * (n - 1 - z) + home * (
        upper * p + (1 - upper) * (n - 1 - p))
    goes_up = jnp.logical_and(z >= p, z < n - 1)
    goes_down = jnp.logical_and(z <= p, z > 0)
    from_below = goes_down
    from_above = goes_up

    def dev(chip, core, node):
        return {"local": 2 * chip + core, "node": node}

    sibling = dev(p, 1 - c, z)
    long_nb, short_nb = dev(ring(s), c, z), dev(ring(-s), c, z)

    def remote(src, dst, send, recv, to):
        return pltpu.make_async_remote_copy(
            src_ref=src, dst_ref=dst, send_sem=send, recv_sem=recv,
            device_id=to, device_id_type=MESH)

    def u_rows(index):
        return pl.ds(pl.multiple_of(index * tok, tok), tok)

    def part(index):
        return pl.ds(pl.multiple_of(index * sub_tok, sub_tok), sub_tok)

    barrier = pltpu.get_barrier_semaphore()
    for k in range(1, n):
        pl.semaphore_signal(barrier, inc=1, device_id=dev(ring(k), c, z), device_id_type=MESH)
    pl.semaphore_signal(barrier, inc=1, device_id=sibling, device_id_type=MESH)

    @pl.when(z > 0)
    def _():
        pl.semaphore_signal(barrier, inc=1, device_id=dev(p, c, z - 1), device_id_type=MESH)

    @pl.when(z < n - 1)
    def _():
        pl.semaphore_signal(barrier, inc=1, device_id=dev(p, c, z + 1), device_id_type=MESH)

    load_w = pltpu.make_async_copy(wrot_ref, w_raw, load_sem.at[0])
    load_w.start()
    load_u = pltpu.make_async_copy(up_ref, u.at[u_rows(l)], load_sem.at[1])
    load_u.start()
    load_x = pltpu.make_async_copy(acts_ref, x.at[p], load_sem.at[2])

    @pl.when(home == 1)
    def _():
        load_x.start()

    pl.semaphore_wait(barrier, n + 2 - lax.div(n - z, n) - lax.div(z + 1, n))

    d1 = remote(acts_ref, x.at[p], d1_send, d1_recv.at[p], dev(z, c, z))

    home_column, home_line = lax.rem(z, 2), lax.div(z, 2)
    home_r = home_column * (n - 1 - home_line) + (1 - home_column) * home_line
    away = lax.rem(s * (r - home_r) + 2 * n, n)
    past = lax.div(away + half - 1, n)
    arc = past * (n - away) + (1 - past) * away
    turn = 2 * (half - arc) + past + lax.div(arc, half)

    @pl.when(jnp.logical_and(home == 0, turn == 1))
    def _():
        d1.start()

    load_u.wait()

    def e_copy_long(step):
        at = u_rows(2 * ring(-s * (step - 1)) + c)
        return remote(u.at[at], u.at[at], e_long.at[step - 1],
                      u_recv.at[2 * ring(-s * (step - 1)) + c], long_nb)

    def e_copy_short(step):
        at = u_rows(2 * ring(s * (step - 1)) + c)
        return remote(u.at[at], u.at[at], e_short.at[step - 1],
                      u_recv.at[2 * ring(s * (step - 1)) + c], short_nb)

    def e_copy_sib(chip):
        at = u_rows(2 * chip + c)
        return remote(u.at[at], u.at[at], e_sib.at[chip], u_recv.at[2 * chip + c], sibling)

    def u_arrived(index):
        pltpu.make_async_copy(u.at[u_rows(index)], u.at[u_rows(index)], u_recv.at[index]).wait()

    e_copy_long(1).start()
    own_rows = pl.ds(pl.multiple_of(c * rows, rows), rows)
    w_copy = remote(w.at[own_rows], w.at[own_rows], w_sem.at[0], w_sem.at[1], sibling)

    def x_chip(i):
        moved = lax.div(i + n - 1, n) * (half - lax.div(i, 2)) * (1 - 2 * lax.rem(i, 2))
        return ring(moved * s)

    def c_chip(i):
        return ring(lax.div(i + 1, 2) * (1 - 2 * lax.rem(i, 2)) * s)

    def x_copy(q, sub, way, node):
        at = part(sub)
        return remote(x.at[q, at], x.at[q, at], x_send.at[way, q * SUB + sub],
                      x_recv.at[q * SUB + sub], dev(p, c, node))

    def xo_copy(q):
        cut = pl.ds(pl.multiple_of((1 - c) * rows, rows), rows)
        return remote(x.at[q, :, cut], xo.at[q], xo_send.at[q], xo_recv.at[q], sibling)

    def c_copy_up(q, sub):
        return remote(pi.at[q, part(sub)], below.at[q, part(sub)], c_send.at[q * SUB + sub],
                      c_recv.at[0, q * SUB + sub], dev(p, c, z + 1))

    def c_copy_down(q, sub):
        return remote(pi.at[q, part(sub)], above.at[q, part(sub)], c_send.at[q * SUB + sub],
                      c_recv.at[1, q * SUB + sub], dev(p, c, z - 1))

    def f_copy(q, sub):
        return remote(pi.at[q, part(sub)], ig_ref.at[part(sub)], f_send.at[q * SUB + sub],
                      f_recv.at[sub], dev(q, c, z))

    def rl_copy(k):
        return remote(po.at[ring(s * k)], rs_long.at[k - 1], rl_send.at[k - 1],
                      rl_recv.at[k - 1], long_nb)

    def rr_copy(k):
        return remote(po.at[ring(-s * k)], rs_short.at[k - 1], rr_send.at[k - 1],
                      rr_recv.at[k - 1], short_nb)

    def rotate(q, index, read):
        at = pl.ds(pl.multiple_of(index * tok, tok), tok)
        for b in range(rows // HBLK):
            turned = lax.dot_general(right_ref[b], read(b), (((1,), (1,)), ((), ())),
                                     preferred_element_type=jnp.float32)
            rot[b * HBLK:(b + 1) * HBLK, at] = (turned * (1.0 / HBLK)).astype(jnp.bfloat16)

    def rotate_own(q):
        rotate(q, 2 * q + c, lambda b: x[
            q, :, pl.ds(pl.multiple_of(c * rows + b * HBLK, HBLK), HBLK)])

    def out_tile(q, tile):
        at = pl.ds(pl.multiple_of(tile * tile_cols, tile_cols), tile_cols)
        po[q, :, at] = jnp.dot(
            x[q], w[:, at], preferred_element_type=jnp.float32).astype(jnp.bfloat16)

    def add_into(total, piece):
        return (total.astype(jnp.float32) + piece.astype(jnp.float32)).astype(jnp.bfloat16)

    c_start = 3
    tile_cols = cols // SUB
    slots = c_start + n - 1 + pieces

    @pl.loop(0, slots)
    def _(t):
        j = t - dist
        i, sub = lax.div(j + SUB, SUB) - 1, lax.rem(j + SUB, SUB)
        here = jnp.logical_and(j >= 0, j < pieces)

        @pl.when(here)
        def _():
            q = x_chip(i)

            @pl.when(jnp.logical_and(home == 1, j == 0))
            def _():
                load_x.wait()

            @pl.when(jnp.logical_and(home == 1, jnp.logical_and(sub == 0, j > 0)))
            def _():
                pltpu.make_async_copy(x.at[q], x.at[q], d1_recv.at[q]).wait()

            @pl.when(home == 0)
            def _():
                pltpu.make_async_copy(x.at[q, part(sub)], x.at[q, part(sub)],
                                      x_recv.at[q * SUB + sub]).wait()

            @pl.when(goes_up)
            def _():
                x_copy(q, sub, 0, z + 1).start()

            @pl.when(goes_down)
            def _():
                x_copy(q, sub, 1, z - 1).start()

            @pl.when(sub == SUB - 1)
            def _():
                xo_copy(q).start()

        jc = t - c_start - c_lag

        @pl.when(jnp.logical_and(jc >= 0, jc < pieces))
        def _():
            sub_c = lax.rem(jc, SUB)
            q = c_chip(lax.div(jc, SUB))
            at = part(sub_c)

            @pl.when(from_below)
            def _():
                pltpu.make_async_copy(below.at[q, at], below.at[q, at],
                                      c_recv.at[0, q * SUB + sub_c]).wait()
                pi[q, at, :] = add_into(pi[q, at, :], below[q, at, :])

            @pl.when(from_above)
            def _():
                pltpu.make_async_copy(above.at[q, at], above.at[q, at],
                                      c_recv.at[1, q * SUB + sub_c]).wait()
                pi[q, at, :] = add_into(pi[q, at, :], above[q, at, :])

            @pl.when(z < p)
            def _():
                c_copy_up(q, sub_c).start()

            @pl.when(z > p)
            def _():
                c_copy_down(q, sub_c).start()

            @pl.when(jnp.logical_and(home == 1, q == p))
            def _():
                ig_ref[at, :] = pi[q, at, :]

            @pl.when(jnp.logical_and(home == 1, q != p))
            def _():
                f_copy(q, sub_c).start()

        @pl.when(t == 0)
        def _():
            load_w.wait()

            @pl.loop(0, rows // HBLK)
            def _(b):
                at = pl.ds(pl.multiple_of(b * HBLK, HBLK), HBLK)
                to = pl.ds(pl.multiple_of(c * rows + b * HBLK, HBLK), HBLK)
                mixed = jnp.dot(left_ref[b], w_raw[at, :], preferred_element_type=jnp.float32)
                w[to, :] = (mixed * (1.0 / HBLK)).astype(jnp.bfloat16)

            w_copy.start()
            e_copy_sib(p).start()

        @pl.when(jnp.logical_and(t == SUB * turn - 5, jnp.logical_and(home == 0, turn > 1)))
        def _():
            d1.start()

        @pl.when(t == 2)
        def _():
            e_copy_short(1).start()

        @pl.when(t == c_start - 1)
        def _():
            w_copy.wait_recv()

        for step in range(1, half + 1):
            @pl.when(t == SUB * (2 * step - 1) + c_start - 1)
            def _(step=step):
                source = ring(-s * step)
                u_arrived(2 * source + c)
                if step < half:
                    e_copy_long(step + 1).start()
                e_copy_sib(source).start()

        for step in range(1, half):
            @pl.when(t == 2 * SUB * step + c_start - 1)
            def _(step=step):
                source = ring(s * step)
                u_arrived(2 * source + c)
                if step < half - 1:
                    e_copy_short(step + 1).start()
                e_copy_sib(source).start()

        jn = jc + 1

        @pl.when(jnp.logical_and(jnp.logical_and(jn >= 0, jn < pieces),
                                 lax.rem(jn + slots * SUB, SUB) == 0))
        def _():
            q = c_chip(lax.div(jn, SUB))

            @pl.loop(0, feats // TILE)
            def _(tile):
                cut = pl.ds(pl.multiple_of(tile * TILE, TILE), TILE)
                pi[q, :, cut] = lax.dot_general(
                    u[u_rows(2 * q + c), :], w[cut, :], (((1,), (1,)), ((), ())),
                    preferred_element_type=jnp.float32).astype(jnp.bfloat16)

        @pl.when(here)
        def _():
            @pl.when(jnp.logical_and(i > 0, sub < 2))
            def _():
                done = x_chip(i - 1)
                for tile in range(SUB // 2):
                    out_tile(done, sub * (SUB // 2) + tile)

            @pl.when(jnp.logical_and(i > 0, sub == 2))
            def _():
                rotate_own(x_chip(i - 1))

            @pl.when(j == pieces - 1)
            def _():
                q = x_chip(n - 1)

                @pl.loop(0, SUB)
                def _(tile):
                    out_tile(q, tile)

        for k in range(half, 0, -1):
            i = 1 if k == half else 2 * (half - k)

            @pl.when(t == n - 1 + SUB * i + SUB + 1)
            def _(k=k):
                if k < half:
                    rl_copy(k + 1).wait_recv()
                    q = ring(s * k)
                    po[q] = add_into(po[q], rs_long[k])
                rl_copy(k).start()

        for k in range(half - 1, 0, -1):
            @pl.when(t == n - 1 + SUB * (2 * (half - k) + 1) + SUB - 1 + 2 * min(k - 1, 1))
            def _(k=k):
                if k < half - 1:
                    rr_copy(k + 1).wait_recv()
                    q = ring(-s * k)
                    po[q] = add_into(po[q], rs_short[k])
                rr_copy(k).start()

    rotate_own(x_chip(n - 1))

    @pl.loop(0, n)
    def _(q):
        pltpu.make_async_copy(xo.at[q], xo.at[q], xo_recv.at[q]).wait()
        u_arrived(2 * q + 1 - c)
        rotate(q, 2 * q + 1 - c, lambda b: xo[q, :, b * HBLK:(b + 1) * HBLK])

    def g_copy(tile, slot):
        at = pl.ds(pl.multiple_of(tile * GRAD_TILE, GRAD_TILE), GRAD_TILE)
        return pltpu.make_async_copy(gt.at[slot], grad_ref.at[:, at], g_sem.at[slot])

    tiles = cols // GRAD_TILE

    @pl.loop(0, tiles)
    def _(tile):
        slot = lax.rem(tile, 2)

        @pl.when(tile >= 2)
        def _():
            g_copy(tile - 2, slot).wait()

        at = pl.ds(pl.multiple_of(tile * GRAD_TILE, GRAD_TILE), GRAD_TILE)
        gt[slot] = jnp.dot(rot[...], u[:, at], preferred_element_type=jnp.float32)
        g_copy(tile, slot).start()

    rl_copy(1).wait_recv()
    rr_copy(1).wait_recv()
    out_ref[...] = (po[p].astype(jnp.float32) + rs_long[0].astype(jnp.float32)
                    + rs_short[0].astype(jnp.float32)).astype(jnp.bfloat16)

    @pl.when(home == 0)
    def _():
        for sub in range(SUB):
            pltpu.make_async_copy(ig_ref.at[part(sub)], ig_ref.at[part(sub)], f_recv.at[sub]).wait()
        d1.wait_send()

    for tile in (tiles - 2, tiles - 1):
        g_copy(tile, tile % 2).wait()
    w_copy.wait_send()
    for step in range(1, half + 1):
        e_copy_long(step).wait_send()
        rl_copy(step).wait_send()
    for step in range(1, half):
        e_copy_short(step).wait_send()
        rr_copy(step).wait_send()

    @pl.loop(0, n)
    def _(q):
        e_copy_sib(q).wait_send()
        xo_copy(q).wait_send()

        @pl.loop(0, SUB)
        def _(sub):
            @pl.when(goes_up)
            def _():
                x_copy(q, sub, 0, z + 1).wait_send()

            @pl.when(goes_down)
            def _():
                x_copy(q, sub, 1, z - 1).wait_send()

            @pl.when(z < p)
            def _():
                c_copy_up(q, sub).wait_send()

            @pl.when(z > p)
            def _():
                c_copy_down(q, sub).wait_send()

            @pl.when(jnp.logical_and(home == 1, q != p))
            def _():
                f_copy(q, sub).wait_send()


COPY_PARTS = 8


def copy_kernel(*refs):
    for source, target in zip(refs[:3], refs[3:]):
        target[...] = source[...]


def hand_on(arrays):
    specs = [pl.BlockSpec((a.shape[0] // COPY_PARTS, a.shape[1]), lambda i: (i, 0)) for a in arrays]
    return pl.pallas_call(
        copy_kernel,
        grid=(COPY_PARTS,),
        out_shape=tuple(jax.ShapeDtypeStruct(a.shape, a.dtype) for a in arrays),
        in_specs=specs,
        out_specs=tuple(specs),
        compiler_params=pltpu.CompilerParams(vmem_limit_bytes=60 << 20),
    )(*arrays)


def fused(acts, w_rot, signs, upstream):
    n = lax.axis_size("node")
    tok, feats = acts.shape
    rows, cols = w_rot.shape
    blocks = rows // HBLK
    half = n // 2
    had = sylvester(HBLK)
    own_signs = lax.dynamic_slice_in_dim(signs, lax.axis_index("local") * rows, rows)
    own_signs = own_signs.astype(jnp.float32).reshape(blocks, HBLK)
    left = (own_signs[:, :, None] * had).astype(jnp.bfloat16)
    right = (own_signs[:, None, :] * had).astype(jnp.bfloat16)
    bf = jnp.bfloat16
    dma = pltpu.SemaphoreType.DMA
    vmem = pl.BlockSpec(memory_space=pltpu.VMEM)
    hbm = pl.BlockSpec(memory_space=pl.ANY)
    tokens = 2 * n * tok
    return hand_on(pl.pallas_call(
        functools.partial(kernel, n),
        out_shape=(
            jax.ShapeDtypeStruct((tok, cols), bf),
            jax.ShapeDtypeStruct((tok, feats), bf),
            jax.ShapeDtypeStruct((rows, cols), jnp.float32),
        ),
        in_specs=[hbm, hbm, hbm, vmem, vmem],
        out_specs=(vmem, vmem, hbm),
        scratch_shapes=[
            pltpu.VMEM((rows, cols), bf),
            pltpu.VMEM((feats, cols), bf),
            pltpu.VMEM((n, tok, feats), bf),
            pltpu.VMEM((n, tok, rows), bf),
            pltpu.VMEM((rows, tokens), bf),
            pltpu.VMEM((tokens, cols), bf),
            pltpu.VMEM((n, tok, feats), bf),
            pltpu.VMEM((n, tok, feats), bf),
            pltpu.VMEM((n, tok, feats), bf),
            pltpu.VMEM((n, tok, cols), bf),
            pltpu.VMEM((half, tok, cols), bf),
            pltpu.VMEM((half - 1, tok, cols), bf),
            pltpu.VMEM((2, rows, GRAD_TILE), jnp.float32),
            dma((3,)), dma, dma((n,)), dma((2, n * SUB)), dma((n * SUB,)), dma((n,)), dma((n,)),
            dma((half,)), dma((half - 1,)), dma((n,)), dma((2 * n,)), dma((2,)),
            dma((n * SUB,)), dma((2, n * SUB)), dma((n * SUB,)), dma((SUB,)),
            dma((half,)), dma((half,)), dma((half - 1,)), dma((half - 1,)), dma((2,)),
        ],
        compiler_params=pltpu.CompilerParams(
            collective_id=0, has_side_effects=True, vmem_limit_bytes=60 << 20),
        cost_estimate=pl.CostEstimate(
            flops=6 * tokens * rows * cols, bytes_accessed=16 * rows * cols, transcendentals=0),
    )(acts, w_rot, upstream, left, right))


def solution(mesh):
    spec = P("local", "node")
    n = mesh.shape["node"]
    paired = mesh.shape["local"] == 2 * n and n >= 4 and n % 2 == 0
    return jax.shard_map(
        fused if paired else local, mesh=mesh, in_specs=(spec, spec, P(), spec),
        out_specs=(spec, spec, spec), check_vma=False,
    )
```

```python
import functools

import jax
import jax.numpy as jnp
from jax import lax
from jax.experimental import pallas as pl
from jax.experimental.pallas import tpu as pltpu
from jax.sharding import PartitionSpec as P

HBLK = 128


def sylvester(order_count):
    row_index = lax.broadcasted_iota(jnp.int32, (order_count, order_count), 0)
    col_index = lax.broadcasted_iota(jnp.int32, (order_count, order_count), 1)
    common = jnp.bitwise_and(row_index, col_index)
    parity = jnp.zeros((order_count, order_count), jnp.int32)
    for bit_index in range(order_count.bit_length() - 1):
        parity = parity + jnp.bitwise_and(jnp.right_shift(common, bit_index), 1)
    return (1 - 2 * jnp.bitwise_and(parity, 1)).astype(jnp.float32)


def local(acts, w_rot, signs, upstream):
    rows, cols = w_rot.shape
    blocks = rows // HBLK
    had = sylvester(HBLK)
    own_signs = lax.dynamic_slice_in_dim(signs, lax.axis_index("local") * rows, rows)
    own_signs = own_signs.astype(jnp.float32).reshape(blocks, HBLK)
    up_all = lax.all_gather(upstream, "local", axis=0, tiled=True)
    feats = lax.all_gather(acts, "node", axis=1, tiled=True)
    own = lax.all_to_all(feats, "local", split_axis=1, concat_axis=0, tiled=True)

    left = (own_signs[:, :, None] * had).astype(jnp.bfloat16)
    mixed = jnp.einsum(
        "bij,bjc->bic", left, w_rot.reshape(blocks, HBLK, cols), preferred_element_type=jnp.float32
    )
    weight = (mixed / HBLK).astype(jnp.bfloat16).reshape(rows, cols)

    terms = lax.dot_general(
        up_all, weight, (((1,), (1,)), ((), ())), preferred_element_type=jnp.float32
    ).astype(jnp.bfloat16)
    terms = lax.all_to_all(terms, "local", split_axis=0, concat_axis=1, tiled=True)
    input_grad = lax.psum_scatter(terms, "node", scatter_dimension=1, tiled=True)

    partial = jnp.dot(own, weight, preferred_element_type=jnp.float32).astype(jnp.bfloat16)
    outputs = lax.psum_scatter(partial, "local", scatter_dimension=0, tiled=True)

    right = (own_signs[:, :, None] * had).astype(jnp.bfloat16)
    rotated = jnp.einsum(
        "tbj,bjk->tbk", own.reshape(-1, blocks, HBLK), right, preferred_element_type=jnp.float32
    )
    rotated = (rotated / HBLK).astype(jnp.bfloat16).reshape(-1, rows)
    grad_rot = lax.dot_general(
        rotated, up_all, (((0,), (0,)), ((), ())), preferred_element_type=jnp.float32
    )
    return outputs, input_grad, grad_rot


SUB = 4
TILE = 512
GRAD_TILE = 256
MESH = pl.DeviceIdType.MESH


def kernel(n, acts_ref, wrot_ref, up_ref, left_ref, right_ref,
           out_ref, ig_ref, grad_ref,
           w, x, xo, rot, u, pi, below, above, po, rs_long, rs_short, g,
           load_sem, d1_send, d1_recv, x_send, x_recv, xo_send, xo_recv,
           e_long, e_short, e_sib, u_recv, w_sem, c_send, c_recv, f_send, f_recv,
           rl_send, rl_recv, rr_send, rr_recv, g_sem):
    half = n // 2
    tok, feats = acts_ref.shape
    rows, cols = wrot_ref.shape
    sub_tok = tok // SUB
    pieces = n * SUB
    l = lax.axis_index("local")
    z = lax.axis_index("node")
    p, c = lax.div(l, 2), lax.rem(l, 2)
    s = 1 - 2 * c
    column, line = lax.rem(p, 2), lax.div(p, 2)
    r = column * (n - 1 - line) + (1 - column) * line

    def ring(offset):
        at = lax.rem(r + offset + 2 * n, n)
        far = lax.div(at, half)
        return (1 - far) * (2 * at) + far * (2 * (n - 1 - at) + 1)

    ge = lax.div(z - p + n, n)
    le = lax.div(p - z + n, n)
    home = ge * le
    dist = (1 - le) * (z - p) + (1 - ge) * (p - z)
    upper = lax.div(2 * p, n)
    c_lag = (1 - ge) * z + (1 - le) * (n - 1 - z) + home * (
        upper * p + (1 - upper) * (n - 1 - p))
    goes_up = jnp.logical_and(z >= p, z < n - 1)
    goes_down = jnp.logical_and(z <= p, z > 0)
    from_below = goes_down
    from_above = goes_up

    def dev(chip, core, node):
        return {"local": 2 * chip + core, "node": node}

    sibling = dev(p, 1 - c, z)
    long_nb, short_nb = dev(ring(s), c, z), dev(ring(-s), c, z)

    def remote(src, dst, send, recv, to):
        return pltpu.make_async_remote_copy(
            src_ref=src, dst_ref=dst, send_sem=send, recv_sem=recv,
            device_id=to, device_id_type=MESH)

    def u_rows(index):
        return pl.ds(pl.multiple_of(index * tok, tok), tok)

    def part(index):
        return pl.ds(pl.multiple_of(index * sub_tok, sub_tok), sub_tok)

    barrier = pltpu.get_barrier_semaphore()
    for k in range(1, n):
        pl.semaphore_signal(barrier, inc=1, device_id=dev(ring(k), c, z), device_id_type=MESH)
    pl.semaphore_signal(barrier, inc=1, device_id=sibling, device_id_type=MESH)

    @pl.when(z > 0)
    def _():
        pl.semaphore_signal(barrier, inc=1, device_id=dev(p, c, z - 1), device_id_type=MESH)

    @pl.when(z < n - 1)
    def _():
        pl.semaphore_signal(barrier, inc=1, device_id=dev(p, c, z + 1), device_id_type=MESH)

    load_u = pltpu.make_async_copy(up_ref, u.at[u_rows(l)], load_sem.at[0])
    load_u.start()
    load_x = pltpu.make_async_copy(acts_ref, x.at[p], load_sem.at[1])
    loads_w = [pltpu.make_async_copy(wrot_ref.at[pl.ds(k * tok, tok)], po.at[k], load_sem.at[2 + k])
               for k in range(rows // tok)]
    for load in loads_w:
        load.start()

    @pl.when(home == 1)
    def _():
        load_x.start()

    pl.semaphore_wait(barrier, n + 2 - lax.div(n - z, n) - lax.div(z + 1, n))

    d1 = remote(acts_ref, x.at[p], d1_send, d1_recv.at[p], dev(z, c, z))

    home_column, home_line = lax.rem(z, 2), lax.div(z, 2)
    home_r = home_column * (n - 1 - home_line) + (1 - home_column) * home_line
    away = lax.rem(s * (r - home_r) + 2 * n, n)
    past = lax.div(away + half - 1, n)
    arc = past * (n - away) + (1 - past) * away
    turn = 2 * (half - arc) + past + lax.div(arc, half)

    @pl.when(jnp.logical_and(home == 0, turn == 1))
    def _():
        d1.start()

    load_u.wait()

    def e_copy_long(step):
        at = u_rows(2 * ring(-s * (step - 1)) + c)
        return remote(u.at[at], u.at[at], e_long.at[step - 1],
                      u_recv.at[2 * ring(-s * (step - 1)) + c], long_nb)

    def e_copy_short(step):
        at = u_rows(2 * ring(s * (step - 1)) + c)
        return remote(u.at[at], u.at[at], e_short.at[step - 1],
                      u_recv.at[2 * ring(s * (step - 1)) + c], short_nb)

    def e_copy_sib(chip):
        at = u_rows(2 * chip + c)
        return remote(u.at[at], u.at[at], e_sib.at[chip], u_recv.at[2 * chip + c], sibling)

    def u_arrived(index):
        pltpu.make_async_copy(u.at[u_rows(index)], u.at[u_rows(index)], u_recv.at[index]).wait()

    e_copy_long(1).start()
    own_rows = pl.ds(pl.multiple_of(c * rows, rows), rows)
    w_copy = remote(w.at[own_rows], w.at[own_rows], w_sem.at[0], w_sem.at[1], sibling)

    def x_chip(i):
        moved = lax.div(i + n - 1, n) * (half - lax.div(i, 2)) * (1 - 2 * lax.rem(i, 2))
        return ring(moved * s)

    def c_chip(i):
        return ring(lax.div(i + 1, 2) * (1 - 2 * lax.rem(i, 2)) * s)

    def x_copy(q, sub, way, node):
        at = part(sub)
        return remote(x.at[q, at], x.at[q, at], x_send.at[way, q * SUB + sub],
                      x_recv.at[q * SUB + sub], dev(p, c, node))

    def xo_copy(q):
        cut = pl.ds(pl.multiple_of((1 - c) * rows, rows), rows)
        return remote(x.at[q, :, cut], xo.at[q], xo_send.at[q], xo_recv.at[q], sibling)

    def c_copy_up(q, sub):
        return remote(pi.at[q, part(sub)], below.at[q, part(sub)], c_send.at[q * SUB + sub],
                      c_recv.at[0, q * SUB + sub], dev(p, c, z + 1))

    def c_copy_down(q, sub):
        return remote(pi.at[q, part(sub)], above.at[q, part(sub)], c_send.at[q * SUB + sub],
                      c_recv.at[1, q * SUB + sub], dev(p, c, z - 1))

    def f_copy(q, sub):
        return remote(pi.at[q, part(sub)], ig_ref.at[part(sub)], f_send.at[q * SUB + sub],
                      f_recv.at[sub], dev(q, c, z))

    def rl_copy(k):
        return remote(po.at[ring(s * k)], rs_long.at[k - 1], rl_send.at[k - 1],
                      rl_recv.at[k - 1], long_nb)

    def rr_copy(k):
        return remote(po.at[ring(-s * k)], rs_short.at[k - 1], rr_send.at[k - 1],
                      rr_recv.at[k - 1], short_nb)

    def rotate(q, index, read):
        at = pl.ds(pl.multiple_of(index * tok, tok), tok)
        for b in range(rows // HBLK):
            turned = lax.dot_general(right_ref[b], read(b), (((1,), (1,)), ((), ())),
                                     preferred_element_type=jnp.float32)
            rot[b * HBLK:(b + 1) * HBLK, at] = (turned * (1.0 / HBLK)).astype(jnp.bfloat16)

    def rotate_own(q):
        rotate(q, 2 * q + c, lambda b: x[
            q, :, pl.ds(pl.multiple_of(c * rows + b * HBLK, HBLK), HBLK)])

    def out_tile(q, tile):
        at = pl.ds(pl.multiple_of(tile * tile_cols, tile_cols), tile_cols)
        po[q, :, at] = jnp.dot(
            x[q], w[:, at], preferred_element_type=jnp.float32).astype(jnp.bfloat16)

    def add_into(total, piece):
        return (total.astype(jnp.float32) + piece.astype(jnp.float32)).astype(jnp.bfloat16)

    c_start = 2
    tile_cols = cols // SUB
    slots = c_start + n - 1 + pieces
    tiles = cols // GRAD_TILE

    def rotate_other(q):
        pltpu.make_async_copy(xo.at[q], xo.at[q], xo_recv.at[q]).wait()
        u_arrived(2 * q + 1 - c)
        rotate(q, 2 * q + 1 - c, lambda b: xo[q, :, b * HBLK:(b + 1) * HBLK])

    def grad_part(q, at):
        both = pl.ds(pl.multiple_of(2 * q * tok, 2 * tok), 2 * tok)
        return jnp.dot(rot[:, both], u[both, at], preferred_element_type=jnp.float32)

    def grad_cols(tile):
        return pl.ds(pl.multiple_of(tile * GRAD_TILE, GRAD_TILE), GRAD_TILE)

    @pl.loop(0, slots)
    def _(t):
        j = t - dist
        i, sub = lax.div(j + SUB, SUB) - 1, lax.rem(j + SUB, SUB)
        here = jnp.logical_and(j >= 0, j < pieces)

        @pl.when(here)
        def _():
            q = x_chip(i)

            @pl.when(jnp.logical_and(home == 1, j == 0))
            def _():
                load_x.wait()

            @pl.when(jnp.logical_and(home == 1, jnp.logical_and(sub == 0, j > 0)))
            def _():
                pltpu.make_async_copy(x.at[q], x.at[q], d1_recv.at[q]).wait()

            @pl.when(home == 0)
            def _():
                pltpu.make_async_copy(x.at[q, part(sub)], x.at[q, part(sub)],
                                      x_recv.at[q * SUB + sub]).wait()

            @pl.when(goes_up)
            def _():
                x_copy(q, sub, 0, z + 1).start()

            @pl.when(goes_down)
            def _():
                x_copy(q, sub, 1, z - 1).start()

            @pl.when(sub == SUB - 1)
            def _():
                xo_copy(q).start()

        jc = t - c_start - c_lag

        @pl.when(jnp.logical_and(jc >= 0, jc < pieces))
        def _():
            sub_c = lax.rem(jc, SUB)
            q = c_chip(lax.div(jc, SUB))
            at = part(sub_c)

            @pl.when(from_below)
            def _():
                pltpu.make_async_copy(below.at[q, at], below.at[q, at],
                                      c_recv.at[0, q * SUB + sub_c]).wait()
                pi[q, at, :] = add_into(pi[q, at, :], below[q, at, :])

            @pl.when(from_above)
            def _():
                pltpu.make_async_copy(above.at[q, at], above.at[q, at],
                                      c_recv.at[1, q * SUB + sub_c]).wait()
                pi[q, at, :] = add_into(pi[q, at, :], above[q, at, :])

            @pl.when(z < p)
            def _():
                c_copy_up(q, sub_c).start()

            @pl.when(z > p)
            def _():
                c_copy_down(q, sub_c).start()

            @pl.when(jnp.logical_and(home == 1, q == p))
            def _():
                ig_ref[at, :] = pi[q, at, :]

            @pl.when(jnp.logical_and(home == 1, q != p))
            def _():
                f_copy(q, sub_c).start()

        @pl.when(t == 0)
        def _():
            for load in loads_w:
                load.wait()

            @pl.loop(0, rows // HBLK)
            def _(b):
                held = tok // HBLK
                at = pl.ds(pl.multiple_of(lax.rem(b, held) * HBLK, HBLK), HBLK)
                to = pl.ds(pl.multiple_of(c * rows + b * HBLK, HBLK), HBLK)
                mixed = jnp.dot(
                    left_ref[b], po[lax.div(b, held), at, :], preferred_element_type=jnp.float32)
                w[to, :] = (mixed * (1.0 / HBLK)).astype(jnp.bfloat16)

            w_copy.start()
            e_copy_sib(p).start()

        @pl.when(jnp.logical_and(t == SUB * turn - 5, jnp.logical_and(home == 0, turn > 1)))
        def _():
            d1.start()

        @pl.when(t == 2)
        def _():
            e_copy_short(1).start()

        @pl.when(t == c_start - 1)
        def _():
            w_copy.wait_recv()

        for step in range(1, half + 1):
            @pl.when(t == SUB * (2 * step - 1) + c_start - 1)
            def _(step=step):
                source = ring(-s * step)
                u_arrived(2 * source + c)
                if step < half:
                    e_copy_long(step + 1).start()
                e_copy_sib(source).start()

        for step in range(1, half):
            @pl.when(t == 2 * SUB * step + c_start - 1)
            def _(step=step):
                source = ring(s * step)
                u_arrived(2 * source + c)
                if step < half - 1:
                    e_copy_short(step + 1).start()
                e_copy_sib(source).start()

        jn = jc + 1

        @pl.when(jnp.logical_and(jnp.logical_and(jn >= 0, jn < pieces),
                                 lax.rem(jn + slots * SUB, SUB) == 0))
        def _():
            q = c_chip(lax.div(jn, SUB))

            @pl.loop(0, feats // TILE)
            def _(tile):
                cut = pl.ds(pl.multiple_of(tile * TILE, TILE), TILE)
                pi[q, :, cut] = lax.dot_general(
                    u[u_rows(2 * q + c), :], w[cut, :], (((1,), (1,)), ((), ())),
                    preferred_element_type=jnp.float32).astype(jnp.bfloat16)

        @pl.when(here)
        def _():
            @pl.when(jnp.logical_and(i > 0, sub < 2))
            def _():
                done = x_chip(i - 1)
                for tile in range(SUB // 2):
                    out_tile(done, sub * (SUB // 2) + tile)

            @pl.when(jnp.logical_and(i > 0, sub == 2))
            def _():
                rotate_own(x_chip(i - 1))

            @pl.when(j == pieces - 1)
            def _():
                q = x_chip(n - 1)

                @pl.loop(0, SUB)
                def _(tile):
                    out_tile(q, tile)

        @pl.when(t == n - 1 + SUB + 3)
        def _():
            rotate_other(p)

            @pl.loop(0, tiles)
            def _(tile):
                at = grad_cols(tile)
                g[:, at] = grad_part(p, at)

        @pl.when(t == n - 1 + SUB * (n - 1) + 2)
        def _():
            across = ring(half)
            rotate_other(across)

            @pl.loop(0, tiles)
            def _(tile):
                at = grad_cols(tile)
                g[:, at] += grad_part(across, at)

        for k in range(half, 0, -1):
            i = 1 if k == half else 2 * (half - k)

            @pl.when(t == n - 1 + SUB * i + SUB + 1)
            def _(k=k):
                if k < half:
                    rl_copy(k + 1).wait_recv()
                    q = ring(s * k)
                    po[q] = add_into(po[q], rs_long[k])
                rl_copy(k).start()

        for k in range(half - 1, 0, -1):
            @pl.when(t == n - 1 + SUB * (2 * (half - k) + 1) + SUB - 1 + 2 * min(k - 1, 1))
            def _(k=k):
                if k < half - 1:
                    rr_copy(k + 1).wait_recv()
                    q = ring(-s * k)
                    po[q] = add_into(po[q], rs_short[k])
                rr_copy(k).start()

    rotate_own(x_chip(n - 1))
    others = [ring(way * k) for k in range(1, half) for way in (1, -1)]
    for q in others:
        rotate_other(q)

    def g_copy(tile):
        at = grad_cols(tile)
        return pltpu.make_async_copy(g.at[:, at], grad_ref.at[:, at], g_sem.at[tile])

    @pl.loop(0, tiles)
    def _(tile):
        at = grad_cols(tile)
        total = g[:, at]
        for q in others:
            total += grad_part(q, at)
        g[:, at] = total
        g_copy(tile).start()

    rl_copy(1).wait_recv()
    rr_copy(1).wait_recv()
    out_ref[...] = (po[p].astype(jnp.float32) + rs_long[0].astype(jnp.float32)
                    + rs_short[0].astype(jnp.float32)).astype(jnp.bfloat16)

    @pl.when(home == 0)
    def _():
        for sub in range(SUB):
            pltpu.make_async_copy(ig_ref.at[part(sub)], ig_ref.at[part(sub)], f_recv.at[sub]).wait()
        d1.wait_send()

    for tile in range(tiles):
        g_copy(tile).wait()
    w_copy.wait_send()
    for step in range(1, half + 1):
        e_copy_long(step).wait_send()
        rl_copy(step).wait_send()
    for step in range(1, half):
        e_copy_short(step).wait_send()
        rr_copy(step).wait_send()

    @pl.loop(0, n)
    def _(q):
        e_copy_sib(q).wait_send()
        xo_copy(q).wait_send()

        @pl.loop(0, SUB)
        def _(sub):
            @pl.when(goes_up)
            def _():
                x_copy(q, sub, 0, z + 1).wait_send()

            @pl.when(goes_down)
            def _():
                x_copy(q, sub, 1, z - 1).wait_send()

            @pl.when(z < p)
            def _():
                c_copy_up(q, sub).wait_send()

            @pl.when(z > p)
            def _():
                c_copy_down(q, sub).wait_send()

            @pl.when(jnp.logical_and(home == 1, q != p))
            def _():
                f_copy(q, sub).wait_send()


COPY_PARTS = 8


def copy_kernel(out_ref, ig_ref, grad_ref, out_to, ig_to, grad_to,
                out_buf, ig_buf, grad_buf, load_sems, store_sems):
    rows = grad_ref.shape[0] // COPY_PARTS
    moves = [(out_ref, out_buf, out_to), (ig_ref, ig_buf, ig_to)]
    for part in range(COPY_PARTS):
        at = pl.ds(part * rows, rows)
        moves.append((grad_ref.at[at], grad_buf.at[at], grad_to.at[at]))
    loads = [pltpu.make_async_copy(source, held, load_sems.at[k])
             for k, (source, held, target) in enumerate(moves)]
    stores = [pltpu.make_async_copy(held, target, store_sems.at[k])
              for k, (source, held, target) in enumerate(moves)]
    for load in loads:
        load.start()
    for load, store in zip(loads, stores):
        load.wait()
        store.start()
    for store in stores:
        store.wait()


def hand_on(arrays):
    hbm = pl.BlockSpec(memory_space=pl.ANY)
    return pl.pallas_call(
        copy_kernel,
        out_shape=tuple(jax.ShapeDtypeStruct(a.shape, a.dtype) for a in arrays),
        in_specs=[hbm] * 3,
        out_specs=(hbm,) * 3,
        scratch_shapes=[pltpu.VMEM(a.shape, a.dtype) for a in arrays]
        + [pltpu.SemaphoreType.DMA((2 + COPY_PARTS,))] * 2,
        compiler_params=pltpu.CompilerParams(vmem_limit_bytes=60 << 20),
    )(*arrays)


def fused(acts, w_rot, signs, upstream):
    n = lax.axis_size("node")
    tok, feats = acts.shape
    rows, cols = w_rot.shape
    blocks = rows // HBLK
    half = n // 2
    had = sylvester(HBLK)
    own_signs = lax.dynamic_slice_in_dim(signs, lax.axis_index("local") * rows, rows)
    own_signs = own_signs.astype(jnp.float32).reshape(blocks, HBLK)
    left = (own_signs[:, :, None] * had).astype(jnp.bfloat16)
    right = (own_signs[:, None, :] * had).astype(jnp.bfloat16)
    bf = jnp.bfloat16
    dma = pltpu.SemaphoreType.DMA
    vmem = pl.BlockSpec(memory_space=pltpu.VMEM)
    hbm = pl.BlockSpec(memory_space=pl.ANY)
    tokens = 2 * n * tok
    return hand_on(pl.pallas_call(
        functools.partial(kernel, n),
        out_shape=(
            jax.ShapeDtypeStruct((tok, cols), bf),
            jax.ShapeDtypeStruct((tok, feats), bf),
            jax.ShapeDtypeStruct((rows, cols), jnp.float32),
        ),
        in_specs=[hbm, hbm, hbm, vmem, vmem],
        out_specs=(vmem, vmem, hbm),
        scratch_shapes=[
            pltpu.VMEM((feats, cols), bf),
            pltpu.VMEM((n, tok, feats), bf),
            pltpu.VMEM((n, tok, rows), bf),
            pltpu.VMEM((rows, tokens), bf),
            pltpu.VMEM((tokens, cols), bf),
            pltpu.VMEM((n, tok, feats), bf),
            pltpu.VMEM((n, tok, feats), bf),
            pltpu.VMEM((n, tok, feats), bf),
            pltpu.VMEM((n, tok, cols), bf),
            pltpu.VMEM((half, tok, cols), bf),
            pltpu.VMEM((half - 1, tok, cols), bf),
            pltpu.VMEM((rows, cols), jnp.float32),
            dma((2 + rows // tok,)), dma, dma((n,)), dma((2, n * SUB)), dma((n * SUB,)), dma((n,)), dma((n,)),
            dma((half,)), dma((half - 1,)), dma((n,)), dma((2 * n,)), dma((2,)),
            dma((n * SUB,)), dma((2, n * SUB)), dma((n * SUB,)), dma((SUB,)),
            dma((half,)), dma((half,)), dma((half - 1,)), dma((half - 1,)), dma((cols // GRAD_TILE,)),
        ],
        compiler_params=pltpu.CompilerParams(
            collective_id=0, has_side_effects=True, vmem_limit_bytes=60 << 20),
        cost_estimate=pl.CostEstimate(
            flops=6 * tokens * rows * cols, bytes_accessed=16 * rows * cols, transcendentals=0),
    )(acts, w_rot, upstream, left, right))


def solution(mesh):
    spec = P("local", "node")
    n = mesh.shape["node"]
    paired = mesh.shape["local"] == 2 * n and n >= 4 and n % 2 == 0
    return jax.shard_map(
        fused if paired else local, mesh=mesh, in_specs=(spec, spec, P(), spec),
        out_specs=(spec, spec, spec), check_vma=False,
    )
```

```python
import functools

import jax
import jax.numpy as jnp
from jax import lax
from jax.experimental import pallas as pl
from jax.experimental.pallas import tpu as pltpu
from jax.sharding import PartitionSpec as P

HBLK = 128


def sylvester(order_count):
    row_index = lax.broadcasted_iota(jnp.int32, (order_count, order_count), 0)
    col_index = lax.broadcasted_iota(jnp.int32, (order_count, order_count), 1)
    common = jnp.bitwise_and(row_index, col_index)
    parity = jnp.zeros((order_count, order_count), jnp.int32)
    for bit_index in range(order_count.bit_length() - 1):
        parity = parity + jnp.bitwise_and(jnp.right_shift(common, bit_index), 1)
    return (1 - 2 * jnp.bitwise_and(parity, 1)).astype(jnp.float32)


def local(acts, w_rot, signs, upstream):
    rows, cols = w_rot.shape
    blocks = rows // HBLK
    had = sylvester(HBLK)
    own_signs = lax.dynamic_slice_in_dim(signs, lax.axis_index("local") * rows, rows)
    own_signs = own_signs.astype(jnp.float32).reshape(blocks, HBLK)
    up_all = lax.all_gather(upstream, "local", axis=0, tiled=True)
    feats = lax.all_gather(acts, "node", axis=1, tiled=True)
    own = lax.all_to_all(feats, "local", split_axis=1, concat_axis=0, tiled=True)

    left = (own_signs[:, :, None] * had).astype(jnp.bfloat16)
    mixed = jnp.einsum(
        "bij,bjc->bic", left, w_rot.reshape(blocks, HBLK, cols), preferred_element_type=jnp.float32
    )
    weight = (mixed / HBLK).astype(jnp.bfloat16).reshape(rows, cols)

    terms = lax.dot_general(
        up_all, weight, (((1,), (1,)), ((), ())), preferred_element_type=jnp.float32
    ).astype(jnp.bfloat16)
    terms = lax.all_to_all(terms, "local", split_axis=0, concat_axis=1, tiled=True)
    input_grad = lax.psum_scatter(terms, "node", scatter_dimension=1, tiled=True)

    partial = jnp.dot(own, weight, preferred_element_type=jnp.float32).astype(jnp.bfloat16)
    outputs = lax.psum_scatter(partial, "local", scatter_dimension=0, tiled=True)

    right = (own_signs[:, :, None] * had).astype(jnp.bfloat16)
    rotated = jnp.einsum(
        "tbj,bjk->tbk", own.reshape(-1, blocks, HBLK), right, preferred_element_type=jnp.float32
    )
    rotated = (rotated / HBLK).astype(jnp.bfloat16).reshape(-1, rows)
    grad_rot = lax.dot_general(
        rotated, up_all, (((0,), (0,)), ((), ())), preferred_element_type=jnp.float32
    )
    return outputs, input_grad, grad_rot


SUB = 8
TILE = 512
GRAD_TILE = 256
MESH = pl.DeviceIdType.MESH


def kernel(n, acts_ref, wrot_ref, up_ref, left_ref, right_ref,
           out_ref, ig_ref, grad_ref,
           w, x, xo, rot, u, pi, below, above, po, rs_long, rs_short, g,
           load_sem, d1_send, d1_recv, x_send, x_recv, xo_send, xo_recv,
           e_long, e_short, e_sib, u_recv, w_sem, c_send, c_recv, f_send, f_recv,
           rl_send, rl_recv, rr_send, rr_recv, g_sem):
    half = n // 2
    tok, feats = acts_ref.shape
    rows, cols = wrot_ref.shape
    sub_tok = tok // SUB
    pieces = n * SUB
    l = lax.axis_index("local")
    z = lax.axis_index("node")
    p, c = lax.div(l, 2), lax.rem(l, 2)
    s = 1 - 2 * c
    column, line = lax.rem(p, 2), lax.div(p, 2)
    r = column * (n - 1 - line) + (1 - column) * line

    def ring(offset):
        at = lax.rem(r + offset + 2 * n, n)
        far = lax.div(at, half)
        return (1 - far) * (2 * at) + far * (2 * (n - 1 - at) + 1)

    ge = lax.div(z - p + n, n)
    le = lax.div(p - z + n, n)
    home = ge * le
    dist = (1 - le) * (z - p) + (1 - ge) * (p - z)
    upper = lax.div(2 * p, n)
    c_lag = (1 - ge) * z + (1 - le) * (n - 1 - z) + home * (
        upper * p + (1 - upper) * (n - 1 - p))
    goes_up = jnp.logical_and(z >= p, z < n - 1)
    goes_down = jnp.logical_and(z <= p, z > 0)
    from_below = goes_down
    from_above = goes_up

    def dev(chip, core, node):
        return {"local": 2 * chip + core, "node": node}

    sibling = dev(p, 1 - c, z)
    long_nb, short_nb = dev(ring(s), c, z), dev(ring(-s), c, z)

    def remote(src, dst, send, recv, to):
        return pltpu.make_async_remote_copy(
            src_ref=src, dst_ref=dst, send_sem=send, recv_sem=recv,
            device_id=to, device_id_type=MESH)

    def u_rows(index):
        return pl.ds(pl.multiple_of(index * tok, tok), tok)

    def part(index):
        return pl.ds(pl.multiple_of(index * sub_tok, sub_tok), sub_tok)

    barrier = pltpu.get_barrier_semaphore()
    for k in range(1, n):
        pl.semaphore_signal(barrier, inc=1, device_id=dev(ring(k), c, z), device_id_type=MESH)
    pl.semaphore_signal(barrier, inc=1, device_id=sibling, device_id_type=MESH)

    @pl.when(z > 0)
    def _():
        pl.semaphore_signal(barrier, inc=1, device_id=dev(p, c, z - 1), device_id_type=MESH)

    @pl.when(z < n - 1)
    def _():
        pl.semaphore_signal(barrier, inc=1, device_id=dev(p, c, z + 1), device_id_type=MESH)

    load_u = pltpu.make_async_copy(up_ref, u.at[u_rows(l)], load_sem.at[0])
    load_u.start()
    load_x = pltpu.make_async_copy(acts_ref, x.at[p], load_sem.at[1])
    loads_w = [pltpu.make_async_copy(wrot_ref.at[pl.ds(k * tok, tok)], po.at[k], load_sem.at[2 + k])
               for k in range(rows // tok)]
    for load in loads_w:
        load.start()

    @pl.when(home == 1)
    def _():
        load_x.start()

    pl.semaphore_wait(barrier, n + 2 - lax.div(n - z, n) - lax.div(z + 1, n))

    d1 = remote(acts_ref, x.at[p], d1_send, d1_recv.at[p], dev(z, c, z))

    home_column, home_line = lax.rem(z, 2), lax.div(z, 2)
    home_r = home_column * (n - 1 - home_line) + (1 - home_column) * home_line
    away = lax.rem(s * (r - home_r) + 2 * n, n)
    past = lax.div(away + half - 1, n)
    arc = past * (n - away) + (1 - past) * away
    turn = 2 * (half - arc) + past + lax.div(arc, half)

    @pl.when(jnp.logical_and(home == 0, turn == 1))
    def _():
        d1.start()

    load_u.wait()

    def e_copy_long(step):
        at = u_rows(2 * ring(-s * (step - 1)) + c)
        return remote(u.at[at], u.at[at], e_long.at[step - 1],
                      u_recv.at[2 * ring(-s * (step - 1)) + c], long_nb)

    def e_copy_short(step):
        at = u_rows(2 * ring(s * (step - 1)) + c)
        return remote(u.at[at], u.at[at], e_short.at[step - 1],
                      u_recv.at[2 * ring(s * (step - 1)) + c], short_nb)

    def e_copy_sib(chip):
        at = u_rows(2 * chip + c)
        return remote(u.at[at], u.at[at], e_sib.at[chip], u_recv.at[2 * chip + c], sibling)

    def u_arrived(index):
        pltpu.make_async_copy(u.at[u_rows(index)], u.at[u_rows(index)], u_recv.at[index]).wait()

    e_copy_long(1).start()
    own_rows = pl.ds(pl.multiple_of(c * rows, rows), rows)
    w_copy = remote(w.at[own_rows], w.at[own_rows], w_sem.at[0], w_sem.at[1], sibling)

    def x_chip(i):
        moved = lax.div(i + n - 1, n) * (half - lax.div(i, 2)) * (1 - 2 * lax.rem(i, 2))
        return ring(moved * s)

    def c_chip(i):
        return ring(lax.div(i + 1, 2) * (1 - 2 * lax.rem(i, 2)) * s)

    def x_copy(q, sub, way, node):
        at = part(sub)
        return remote(x.at[q, at], x.at[q, at], x_send.at[way, q * SUB + sub],
                      x_recv.at[q * SUB + sub], dev(p, c, node))

    def xo_copy(q):
        cut = pl.ds(pl.multiple_of((1 - c) * rows, rows), rows)
        return remote(x.at[q, :, cut], xo.at[q], xo_send.at[q], xo_recv.at[q], sibling)

    def c_copy_up(q, sub):
        return remote(pi.at[q, part(sub)], below.at[q, part(sub)], c_send.at[q * SUB + sub],
                      c_recv.at[0, q * SUB + sub], dev(p, c, z + 1))

    def c_copy_down(q, sub):
        return remote(pi.at[q, part(sub)], above.at[q, part(sub)], c_send.at[q * SUB + sub],
                      c_recv.at[1, q * SUB + sub], dev(p, c, z - 1))

    def f_copy(q, sub):
        return remote(pi.at[q, part(sub)], ig_ref.at[part(sub)], f_send.at[q * SUB + sub],
                      f_recv.at[sub], dev(q, c, z))

    def rl_copy(k):
        return remote(po.at[ring(s * k)], rs_long.at[k - 1], rl_send.at[k - 1],
                      rl_recv.at[k - 1], long_nb)

    def rr_copy(k):
        return remote(po.at[ring(-s * k)], rs_short.at[k - 1], rr_send.at[k - 1],
                      rr_recv.at[k - 1], short_nb)

    def rotate(q, index, read):
        at = pl.ds(pl.multiple_of(index * tok, tok), tok)
        for b in range(rows // HBLK):
            turned = lax.dot_general(right_ref[b], read(b), (((1,), (1,)), ((), ())),
                                     preferred_element_type=jnp.float32)
            rot[b * HBLK:(b + 1) * HBLK, at] = (turned * (1.0 / HBLK)).astype(jnp.bfloat16)

    def rotate_own(q):
        rotate(q, 2 * q + c, lambda b: x[
            q, :, pl.ds(pl.multiple_of(c * rows + b * HBLK, HBLK), HBLK)])

    def out_tile(q, tile):
        at = pl.ds(pl.multiple_of(tile * tile_cols, tile_cols), tile_cols)
        po[q, :, at] = jnp.dot(
            x[q], w[:, at], preferred_element_type=jnp.float32).astype(jnp.bfloat16)

    def add_into(total, piece):
        return (total.astype(jnp.float32) + piece.astype(jnp.float32)).astype(jnp.bfloat16)

    c_start = 4
    tile_cols = cols // SUB
    slots = c_start + n - 1 + pieces
    tiles = cols // GRAD_TILE

    def rotate_other(q):
        pltpu.make_async_copy(xo.at[q], xo.at[q], xo_recv.at[q]).wait()
        u_arrived(2 * q + 1 - c)
        rotate(q, 2 * q + 1 - c, lambda b: xo[q, :, b * HBLK:(b + 1) * HBLK])

    def grad_part(q, at):
        both = pl.ds(pl.multiple_of(2 * q * tok, 2 * tok), 2 * tok)
        return jnp.dot(rot[:, both], u[both, at], preferred_element_type=jnp.float32)

    def grad_cols(tile):
        return pl.ds(pl.multiple_of(tile * GRAD_TILE, GRAD_TILE), GRAD_TILE)

    @pl.loop(0, slots)
    def _(t):
        j = t - dist
        i, sub = lax.div(j + SUB, SUB) - 1, lax.rem(j + SUB, SUB)
        here = jnp.logical_and(j >= 0, j < pieces)

        @pl.when(here)
        def _():
            q = x_chip(i)

            @pl.when(jnp.logical_and(home == 1, j == 0))
            def _():
                load_x.wait()

            @pl.when(jnp.logical_and(home == 1, jnp.logical_and(sub == 0, j > 0)))
            def _():
                pltpu.make_async_copy(x.at[q], x.at[q], d1_recv.at[q]).wait()

            @pl.when(home == 0)
            def _():
                pltpu.make_async_copy(x.at[q, part(sub)], x.at[q, part(sub)],
                                      x_recv.at[q * SUB + sub]).wait()

            @pl.when(goes_up)
            def _():
                x_copy(q, sub, 0, z + 1).start()

            @pl.when(goes_down)
            def _():
                x_copy(q, sub, 1, z - 1).start()

            @pl.when(sub == SUB - 1)
            def _():
                xo_copy(q).start()

        jc = t - c_start - c_lag

        @pl.when(jnp.logical_and(jc >= 0, jc < pieces))
        def _():
            sub_c = lax.rem(jc, SUB)
            q = c_chip(lax.div(jc, SUB))
            at = part(sub_c)

            @pl.when(from_below)
            def _():
                pltpu.make_async_copy(below.at[q, at], below.at[q, at],
                                      c_recv.at[0, q * SUB + sub_c]).wait()
                pi[q, at, :] = add_into(pi[q, at, :], below[q, at, :])

            @pl.when(from_above)
            def _():
                pltpu.make_async_copy(above.at[q, at], above.at[q, at],
                                      c_recv.at[1, q * SUB + sub_c]).wait()
                pi[q, at, :] = add_into(pi[q, at, :], above[q, at, :])

            @pl.when(z < p)
            def _():
                c_copy_up(q, sub_c).start()

            @pl.when(z > p)
            def _():
                c_copy_down(q, sub_c).start()

            @pl.when(jnp.logical_and(home == 1, q == p))
            def _():
                ig_ref[at, :] = pi[q, at, :]

            @pl.when(jnp.logical_and(home == 1, q != p))
            def _():
                f_copy(q, sub_c).start()

        @pl.when(t == 0)
        def _():
            for load in loads_w:
                load.wait()

            @pl.loop(0, rows // HBLK)
            def _(b):
                held = tok // HBLK
                at = pl.ds(pl.multiple_of(lax.rem(b, held) * HBLK, HBLK), HBLK)
                to = pl.ds(pl.multiple_of(c * rows + b * HBLK, HBLK), HBLK)
                mixed = jnp.dot(
                    left_ref[b], po[lax.div(b, held), at, :], preferred_element_type=jnp.float32)
                w[to, :] = (mixed * (1.0 / HBLK)).astype(jnp.bfloat16)

            w_copy.start()
            e_copy_sib(p).start()

        @pl.when(jnp.logical_and(t == SUB * turn - 12, jnp.logical_and(home == 0, turn > 1)))
        def _():
            d1.start()

        @pl.when(t == 3)
        def _():
            e_copy_short(1).start()

        @pl.when(t == c_start - 1)
        def _():
            w_copy.wait_recv()

        for step in range(1, half + 1):
            @pl.when(t == SUB * (2 * step - 1) + c_start - 1)
            def _(step=step):
                source = ring(-s * step)
                u_arrived(2 * source + c)
                if step < half:
                    e_copy_long(step + 1).start()
                e_copy_sib(source).start()

        for step in range(1, half):
            @pl.when(t == 2 * SUB * step + c_start - 1)
            def _(step=step):
                source = ring(s * step)
                u_arrived(2 * source + c)
                if step < half - 1:
                    e_copy_short(step + 1).start()
                e_copy_sib(source).start()

        jn = jc + 1

        @pl.when(jnp.logical_and(jnp.logical_and(jn >= 0, jn < pieces),
                                 lax.rem(jn + slots * SUB, SUB) == 0))
        def _():
            q = c_chip(lax.div(jn, SUB))

            @pl.loop(0, feats // TILE)
            def _(tile):
                cut = pl.ds(pl.multiple_of(tile * TILE, TILE), TILE)
                pi[q, :, cut] = lax.dot_general(
                    u[u_rows(2 * q + c), :], w[cut, :], (((1,), (1,)), ((), ())),
                    preferred_element_type=jnp.float32).astype(jnp.bfloat16)

        @pl.when(here)
        def _():
            @pl.when(jnp.logical_and(i > 0, sub < 2))
            def _():
                done = x_chip(i - 1)
                for tile in range(SUB // 2):
                    out_tile(done, sub * (SUB // 2) + tile)

            @pl.when(jnp.logical_and(i > 0, sub == 2))
            def _():
                rotate_own(x_chip(i - 1))

            @pl.when(j == pieces - 1)
            def _():
                q = x_chip(n - 1)

                @pl.loop(0, SUB)
                def _(tile):
                    out_tile(q, tile)

        @pl.when(t == n - 1 + SUB + 3)
        def _():
            rotate_other(p)

            @pl.loop(0, tiles)
            def _(tile):
                at = grad_cols(tile)
                g[:, at] = grad_part(p, at)

        @pl.when(t == n - 1 + SUB * (n - 1) + 2)
        def _():
            across = ring(half)
            rotate_other(across)

            @pl.loop(0, tiles)
            def _(tile):
                at = grad_cols(tile)
                g[:, at] += grad_part(across, at)

        for k in range(half, 0, -1):
            i = 1 if k == half else 2 * (half - k)

            @pl.when(t == n - 1 + SUB * i + SUB + 1)
            def _(k=k):
                if k < half:
                    rl_copy(k + 1).wait_recv()
                    q = ring(s * k)
                    po[q] = add_into(po[q], rs_long[k])
                rl_copy(k).start()

        for k in range(half - 1, 0, -1):
            @pl.when(t == n - 1 + SUB * (2 * (half - k) + 1) + SUB - 1 + 2 * min(k - 1, 1))
            def _(k=k):
                if k < half - 1:
                    rr_copy(k + 1).wait_recv()
                    q = ring(-s * k)
                    po[q] = add_into(po[q], rs_short[k])
                rr_copy(k).start()

    rotate_own(x_chip(n - 1))
    others = [ring(way * k) for k in range(1, half) for way in (1, -1)]
    for q in others:
        rotate_other(q)

    def g_copy(tile):
        at = grad_cols(tile)
        return pltpu.make_async_copy(g.at[:, at], grad_ref.at[:, at], g_sem.at[tile])

    @pl.loop(0, tiles)
    def _(tile):
        at = grad_cols(tile)
        total = g[:, at]
        for q in others:
            total += grad_part(q, at)
        g[:, at] = total
        g_copy(tile).start()

    rl_copy(1).wait_recv()
    rr_copy(1).wait_recv()
    out_ref[...] = (po[p].astype(jnp.float32) + rs_long[0].astype(jnp.float32)
                    + rs_short[0].astype(jnp.float32)).astype(jnp.bfloat16)

    @pl.when(home == 0)
    def _():
        for sub in range(SUB):
            pltpu.make_async_copy(ig_ref.at[part(sub)], ig_ref.at[part(sub)], f_recv.at[sub]).wait()
        d1.wait_send()

    for tile in range(tiles):
        g_copy(tile).wait()
    w_copy.wait_send()
    for step in range(1, half + 1):
        e_copy_long(step).wait_send()
        rl_copy(step).wait_send()
    for step in range(1, half):
        e_copy_short(step).wait_send()
        rr_copy(step).wait_send()

    @pl.loop(0, n)
    def _(q):
        e_copy_sib(q).wait_send()
        xo_copy(q).wait_send()

        @pl.loop(0, SUB)
        def _(sub):
            @pl.when(goes_up)
            def _():
                x_copy(q, sub, 0, z + 1).wait_send()

            @pl.when(goes_down)
            def _():
                x_copy(q, sub, 1, z - 1).wait_send()

            @pl.when(z < p)
            def _():
                c_copy_up(q, sub).wait_send()

            @pl.when(z > p)
            def _():
                c_copy_down(q, sub).wait_send()

            @pl.when(jnp.logical_and(home == 1, q != p))
            def _():
                f_copy(q, sub).wait_send()


COPY_PARTS = 8


def copy_kernel(out_ref, ig_ref, grad_ref, out_to, ig_to, grad_to,
                out_buf, ig_buf, grad_buf, load_sems, store_sems):
    rows = grad_ref.shape[0] // COPY_PARTS
    moves = [(out_ref, out_buf, out_to), (ig_ref, ig_buf, ig_to)]
    for part in range(COPY_PARTS):
        at = pl.ds(part * rows, rows)
        moves.append((grad_ref.at[at], grad_buf.at[at], grad_to.at[at]))
    loads = [pltpu.make_async_copy(source, held, load_sems.at[k])
             for k, (source, held, target) in enumerate(moves)]
    stores = [pltpu.make_async_copy(held, target, store_sems.at[k])
              for k, (source, held, target) in enumerate(moves)]
    for load in loads:
        load.start()
    for load, store in zip(loads, stores):
        load.wait()
        store.start()
    for store in stores:
        store.wait()


def hand_on(arrays):
    hbm = pl.BlockSpec(memory_space=pl.ANY)
    return pl.pallas_call(
        copy_kernel,
        out_shape=tuple(jax.ShapeDtypeStruct(a.shape, a.dtype) for a in arrays),
        in_specs=[hbm] * 3,
        out_specs=(hbm,) * 3,
        scratch_shapes=[pltpu.VMEM(a.shape, a.dtype) for a in arrays]
        + [pltpu.SemaphoreType.DMA((2 + COPY_PARTS,))] * 2,
        compiler_params=pltpu.CompilerParams(vmem_limit_bytes=60 << 20),
    )(*arrays)


def fused(acts, w_rot, signs, upstream):
    n = lax.axis_size("node")
    tok, feats = acts.shape
    rows, cols = w_rot.shape
    blocks = rows // HBLK
    half = n // 2
    had = sylvester(HBLK)
    own_signs = lax.dynamic_slice_in_dim(signs, lax.axis_index("local") * rows, rows)
    own_signs = own_signs.astype(jnp.float32).reshape(blocks, HBLK)
    left = (own_signs[:, :, None] * had).astype(jnp.bfloat16)
    right = (own_signs[:, None, :] * had).astype(jnp.bfloat16)
    bf = jnp.bfloat16
    dma = pltpu.SemaphoreType.DMA
    vmem = pl.BlockSpec(memory_space=pltpu.VMEM)
    hbm = pl.BlockSpec(memory_space=pl.ANY)
    tokens = 2 * n * tok
    return hand_on(pl.pallas_call(
        functools.partial(kernel, n),
        out_shape=(
            jax.ShapeDtypeStruct((tok, cols), bf),
            jax.ShapeDtypeStruct((tok, feats), bf),
            jax.ShapeDtypeStruct((rows, cols), jnp.float32),
        ),
        in_specs=[hbm, hbm, hbm, vmem, vmem],
        out_specs=(vmem, vmem, hbm),
        scratch_shapes=[
            pltpu.VMEM((feats, cols), bf),
            pltpu.VMEM((n, tok, feats), bf),
            pltpu.VMEM((n, tok, rows), bf),
            pltpu.VMEM((rows, tokens), bf),
            pltpu.VMEM((tokens, cols), bf),
            pltpu.VMEM((n, tok, feats), bf),
            pltpu.VMEM((n, tok, feats), bf),
            pltpu.VMEM((n, tok, feats), bf),
            pltpu.VMEM((n, tok, cols), bf),
            pltpu.VMEM((half, tok, cols), bf),
            pltpu.VMEM((half - 1, tok, cols), bf),
            pltpu.VMEM((rows, cols), jnp.float32),
            dma((2 + rows // tok,)), dma, dma((n,)), dma((2, n * SUB)), dma((n * SUB,)), dma((n,)), dma((n,)),
            dma((half,)), dma((half - 1,)), dma((n,)), dma((2 * n,)), dma((2,)),
            dma((n * SUB,)), dma((2, n * SUB)), dma((n * SUB,)), dma((SUB,)),
            dma((half,)), dma((half,)), dma((half - 1,)), dma((half - 1,)), dma((cols // GRAD_TILE,)),
        ],
        compiler_params=pltpu.CompilerParams(
            collective_id=0, has_side_effects=True, vmem_limit_bytes=60 << 20),
        cost_estimate=pl.CostEstimate(
            flops=6 * tokens * rows * cols, bytes_accessed=16 * rows * cols, transcendentals=0),
    )(acts, w_rot, upstream, left, right))


def solution(mesh):
    spec = P("local", "node")
    n = mesh.shape["node"]
    paired = mesh.shape["local"] == 2 * n and n >= 4 and n % 2 == 0
    return jax.shard_map(
        fused if paired else local, mesh=mesh, in_specs=(spec, spec, P(), spec),
        out_specs=(spec, spec, spec), check_vma=False,
    )
```

```python
import functools

import jax
import jax.numpy as jnp
from jax import lax
from jax.experimental import pallas as pl
from jax.experimental.pallas import tpu as pltpu
from jax.sharding import PartitionSpec as P

HBLK = 128


def sylvester(order_count):
    row_index = lax.broadcasted_iota(jnp.int32, (order_count, order_count), 0)
    col_index = lax.broadcasted_iota(jnp.int32, (order_count, order_count), 1)
    common = jnp.bitwise_and(row_index, col_index)
    parity = jnp.zeros((order_count, order_count), jnp.int32)
    for bit_index in range(order_count.bit_length() - 1):
        parity = parity + jnp.bitwise_and(jnp.right_shift(common, bit_index), 1)
    return (1 - 2 * jnp.bitwise_and(parity, 1)).astype(jnp.float32)


def local(acts, w_rot, signs, upstream):
    rows, cols = w_rot.shape
    blocks = rows // HBLK
    had = sylvester(HBLK)
    own_signs = lax.dynamic_slice_in_dim(signs, lax.axis_index("local") * rows, rows)
    own_signs = own_signs.astype(jnp.float32).reshape(blocks, HBLK)
    up_all = lax.all_gather(upstream, "local", axis=0, tiled=True)
    feats = lax.all_gather(acts, "node", axis=1, tiled=True)
    own = lax.all_to_all(feats, "local", split_axis=1, concat_axis=0, tiled=True)

    left = (own_signs[:, :, None] * had).astype(jnp.bfloat16)
    mixed = jnp.einsum(
        "bij,bjc->bic", left, w_rot.reshape(blocks, HBLK, cols), preferred_element_type=jnp.float32
    )
    weight = (mixed / HBLK).astype(jnp.bfloat16).reshape(rows, cols)

    terms = lax.dot_general(
        up_all, weight, (((1,), (1,)), ((), ())), preferred_element_type=jnp.float32
    ).astype(jnp.bfloat16)
    terms = lax.all_to_all(terms, "local", split_axis=0, concat_axis=1, tiled=True)
    input_grad = lax.psum_scatter(terms, "node", scatter_dimension=1, tiled=True)

    partial = jnp.dot(own, weight, preferred_element_type=jnp.float32).astype(jnp.bfloat16)
    outputs = lax.psum_scatter(partial, "local", scatter_dimension=0, tiled=True)

    right = (own_signs[:, :, None] * had).astype(jnp.bfloat16)
    rotated = jnp.einsum(
        "tbj,bjk->tbk", own.reshape(-1, blocks, HBLK), right, preferred_element_type=jnp.float32
    )
    rotated = (rotated / HBLK).astype(jnp.bfloat16).reshape(-1, rows)
    grad_rot = lax.dot_general(
        rotated, up_all, (((0,), (0,)), ((), ())), preferred_element_type=jnp.float32
    )
    return outputs, input_grad, grad_rot


SUB = 4
TILE = 512
GRAD_TILE = 256
MESH = pl.DeviceIdType.MESH


def kernel(n, acts_ref, wrot_ref, up_ref, left_ref, right_ref,
           out_ref, ig_ref, grad_ref,
           w, x, xo, rot, u, pi, below, above, po, rs_long, rs_short, g,
           load_sem, d1_send, d1_recv, x_send, x_recv, xo_send, xo_recv,
           e_long, e_short, e_sib, u_recv, w_sem, c_send, c_recv, f_send, f_recv,
           rl_send, rl_recv, rr_send, rr_recv, g_sem):
    half = n // 2
    tok, feats = acts_ref.shape
    rows, cols = wrot_ref.shape
    sub_tok = tok // SUB
    pieces = n * SUB
    l = lax.axis_index("local")
    z = lax.axis_index("node")
    p, c = lax.div(l, 2), lax.rem(l, 2)
    s = 1 - 2 * c
    column, line = lax.rem(p, 2), lax.div(p, 2)
    r = column * (n - 1 - line) + (1 - column) * line

    def ring(offset):
        at = lax.rem(r + offset + 2 * n, n)
        far = lax.div(at, half)
        return (1 - far) * (2 * at) + far * (2 * (n - 1 - at) + 1)

    ge = lax.div(z - p + n, n)
    le = lax.div(p - z + n, n)
    home = ge * le
    dist = (1 - le) * (z - p) + (1 - ge) * (p - z)
    upper = lax.div(2 * p, n)
    c_lag = (1 - ge) * z + (1 - le) * (n - 1 - z) + home * (
        upper * p + (1 - upper) * (n - 1 - p))
    goes_up = jnp.logical_and(z >= p, z < n - 1)
    goes_down = jnp.logical_and(z <= p, z > 0)
    from_below = goes_down
    from_above = goes_up

    def dev(chip, core, node):
        return {"local": 2 * chip + core, "node": node}

    sibling = dev(p, 1 - c, z)
    long_nb, short_nb = dev(ring(s), c, z), dev(ring(-s), c, z)

    def remote(src, dst, send, recv, to):
        return pltpu.make_async_remote_copy(
            src_ref=src, dst_ref=dst, send_sem=send, recv_sem=recv,
            device_id=to, device_id_type=MESH)

    def u_rows(index):
        return pl.ds(pl.multiple_of(index * tok, tok), tok)

    def part(index):
        return pl.ds(pl.multiple_of(index * sub_tok, sub_tok), sub_tok)

    barrier = pltpu.get_barrier_semaphore()
    for k in range(1, n):
        pl.semaphore_signal(barrier, inc=1, device_id=dev(ring(k), c, z), device_id_type=MESH)
    pl.semaphore_signal(barrier, inc=1, device_id=sibling, device_id_type=MESH)

    @pl.when(z > 0)
    def _():
        pl.semaphore_signal(barrier, inc=1, device_id=dev(p, c, z - 1), device_id_type=MESH)

    @pl.when(z < n - 1)
    def _():
        pl.semaphore_signal(barrier, inc=1, device_id=dev(p, c, z + 1), device_id_type=MESH)

    load_u = pltpu.make_async_copy(up_ref, u.at[u_rows(l)], load_sem.at[0])
    load_u.start()
    load_x = pltpu.make_async_copy(acts_ref, x.at[p], load_sem.at[1])
    loads_w = [pltpu.make_async_copy(wrot_ref.at[pl.ds(k * tok, tok)], po.at[k], load_sem.at[2 + k])
               for k in range(rows // tok)]
    for load in loads_w:
        load.start()

    @pl.when(home == 1)
    def _():
        load_x.start()

    pl.semaphore_wait(barrier, n + 2 - lax.div(n - z, n) - lax.div(z + 1, n))

    d1 = remote(acts_ref, x.at[p], d1_send, d1_recv.at[p], dev(z, c, z))

    home_column, home_line = lax.rem(z, 2), lax.div(z, 2)
    home_r = home_column * (n - 1 - home_line) + (1 - home_column) * home_line
    away = lax.rem(s * (r - home_r) + 2 * n, n)
    past = lax.div(away + half - 1, n)
    arc = past * (n - away) + (1 - past) * away
    turn = 2 * (half - arc) + past + lax.div(arc, half)

    @pl.when(jnp.logical_and(home == 0, turn == 1))
    def _():
        d1.start()

    load_u.wait()

    def e_copy_long(step):
        at = u_rows(2 * ring(-s * (step - 1)) + c)
        return remote(u.at[at], u.at[at], e_long.at[step - 1],
                      u_recv.at[2 * ring(-s * (step - 1)) + c], long_nb)

    def e_copy_short(step):
        at = u_rows(2 * ring(s * (step - 1)) + c)
        return remote(u.at[at], u.at[at], e_short.at[step - 1],
                      u_recv.at[2 * ring(s * (step - 1)) + c], short_nb)

    def e_copy_sib(chip):
        at = u_rows(2 * chip + c)
        return remote(u.at[at], u.at[at], e_sib.at[chip], u_recv.at[2 * chip + c], sibling)

    def u_arrived(index):
        pltpu.make_async_copy(u.at[u_rows(index)], u.at[u_rows(index)], u_recv.at[index]).wait()

    e_copy_long(1).start()
    own_rows = pl.ds(pl.multiple_of(c * rows, rows), rows)
    w_copy = remote(w.at[own_rows], w.at[own_rows], w_sem.at[0], w_sem.at[1], sibling)

    def x_chip(i):
        moved = lax.div(i + n - 1, n) * (half - lax.div(i, 2)) * (1 - 2 * lax.rem(i, 2))
        return ring(moved * s)

    def c_chip(i):
        return ring(lax.div(i + 1, 2) * (1 - 2 * lax.rem(i, 2)) * s)

    def x_copy(q, sub, way, node):
        at = part(sub)
        return remote(x.at[q, at], x.at[q, at], x_send.at[way, q * SUB + sub],
                      x_recv.at[q * SUB + sub], dev(p, c, node))

    def xo_copy(q):
        cut = pl.ds(pl.multiple_of((1 - c) * rows, rows), rows)
        return remote(x.at[q, :, cut], xo.at[q], xo_send.at[q], xo_recv.at[q], sibling)

    def c_copy_up(q, sub):
        return remote(pi.at[q, part(sub)], below.at[q, part(sub)], c_send.at[q * SUB + sub],
                      c_recv.at[0, q * SUB + sub], dev(p, c, z + 1))

    def c_copy_down(q, sub):
        return remote(pi.at[q, part(sub)], above.at[q, part(sub)], c_send.at[q * SUB + sub],
                      c_recv.at[1, q * SUB + sub], dev(p, c, z - 1))

    def f_copy(q, sub):
        return remote(pi.at[q, part(sub)], ig_ref.at[part(sub)], f_send.at[q * SUB + sub],
                      f_recv.at[sub], dev(q, c, z))

    def rl_copy(k):
        return remote(po.at[ring(s * k)], rs_long.at[k - 1], rl_send.at[k - 1],
                      rl_recv.at[k - 1], long_nb)

    def rr_copy(k):
        return remote(po.at[ring(-s * k)], rs_short.at[k - 1], rr_send.at[k - 1],
                      rr_recv.at[k - 1], short_nb)

    def rotate(q, index, read):
        at = pl.ds(pl.multiple_of(index * tok, tok), tok)
        for b in range(rows // HBLK):
            turned = lax.dot_general(right_ref[b], read(b), (((1,), (1,)), ((), ())),
                                     preferred_element_type=jnp.float32)
            rot[b * HBLK:(b + 1) * HBLK, at] = (turned * (1.0 / HBLK)).astype(jnp.bfloat16)

    def rotate_own(q):
        rotate(q, 2 * q + c, lambda b: x[
            q, :, pl.ds(pl.multiple_of(c * rows + b * HBLK, HBLK), HBLK)])

    def out_tile(q, tile):
        at = pl.ds(pl.multiple_of(tile * tile_cols, tile_cols), tile_cols)
        po[q, :, at] = jnp.dot(
            x[q], w[:, at], preferred_element_type=jnp.float32).astype(jnp.bfloat16)

    def add_into(total, piece):
        return (total.astype(jnp.float32) + piece.astype(jnp.float32)).astype(jnp.bfloat16)

    c_start = 2
    tile_cols = cols // SUB
    slots = c_start + n - 1 + pieces
    tiles = cols // GRAD_TILE

    def rotate_other(q):
        pltpu.make_async_copy(xo.at[q], xo.at[q], xo_recv.at[q]).wait()
        u_arrived(2 * q + 1 - c)
        rotate(q, 2 * q + 1 - c, lambda b: xo[q, :, b * HBLK:(b + 1) * HBLK])

    def grad_part(q, at):
        both = pl.ds(pl.multiple_of(2 * q * tok, 2 * tok), 2 * tok)
        return jnp.dot(rot[:, both], u[both, at], preferred_element_type=jnp.float32)

    def grad_cols(tile):
        return pl.ds(pl.multiple_of(tile * GRAD_TILE, GRAD_TILE), GRAD_TILE)

    @pl.loop(0, slots)
    def _(t):
        j = t - dist
        i, sub = lax.div(j + SUB, SUB) - 1, lax.rem(j + SUB, SUB)
        here = jnp.logical_and(j >= 0, j < pieces)

        @pl.when(here)
        def _():
            q = x_chip(i)

            @pl.when(jnp.logical_and(home == 1, j == 0))
            def _():
                load_x.wait()

            @pl.when(jnp.logical_and(home == 1, jnp.logical_and(sub == 0, j > 0)))
            def _():
                pltpu.make_async_copy(x.at[q], x.at[q], d1_recv.at[q]).wait()

            @pl.when(home == 0)
            def _():
                pltpu.make_async_copy(x.at[q, part(sub)], x.at[q, part(sub)],
                                      x_recv.at[q * SUB + sub]).wait()

            @pl.when(goes_up)
            def _():
                x_copy(q, sub, 0, z + 1).start()

            @pl.when(goes_down)
            def _():
                x_copy(q, sub, 1, z - 1).start()

            @pl.when(sub == SUB - 1)
            def _():
                xo_copy(q).start()

        jc = t - c_start - c_lag

        @pl.when(jnp.logical_and(jc >= 0, jc < pieces))
        def _():
            sub_c = lax.rem(jc, SUB)
            q = c_chip(lax.div(jc, SUB))
            at = part(sub_c)

            @pl.when(from_below)
            def _():
                pltpu.make_async_copy(below.at[q, at], below.at[q, at],
                                      c_recv.at[0, q * SUB + sub_c]).wait()
                pi[q, at, :] = add_into(pi[q, at, :], below[q, at, :])

            @pl.when(from_above)
            def _():
                pltpu.make_async_copy(above.at[q, at], above.at[q, at],
                                      c_recv.at[1, q * SUB + sub_c]).wait()
                pi[q, at, :] = add_into(pi[q, at, :], above[q, at, :])

            @pl.when(z < p)
            def _():
                c_copy_up(q, sub_c).start()

            @pl.when(z > p)
            def _():
                c_copy_down(q, sub_c).start()

            @pl.when(jnp.logical_and(home == 1, q == p))
            def _():
                ig_ref[at, :] = pi[q, at, :]

            @pl.when(jnp.logical_and(home == 1, q != p))
            def _():
                f_copy(q, sub_c).start()

        @pl.when(t == 0)
        def _():
            for load in loads_w:
                load.wait()

            @pl.loop(0, rows // HBLK)
            def _(b):
                held = tok // HBLK
                at = pl.ds(pl.multiple_of(lax.rem(b, held) * HBLK, HBLK), HBLK)
                to = pl.ds(pl.multiple_of(c * rows + b * HBLK, HBLK), HBLK)
                mixed = jnp.dot(
                    left_ref[b], po[lax.div(b, held), at, :], preferred_element_type=jnp.float32)
                w[to, :] = (mixed * (1.0 / HBLK)).astype(jnp.bfloat16)

            w_copy.start()
            e_copy_sib(p).start()

        @pl.when(jnp.logical_and(t == SUB * turn - 8, jnp.logical_and(home == 0, turn > 1)))
        def _():
            d1.start()

        @pl.when(t == 2)
        def _():
            e_copy_short(1).start()

        @pl.when(t == c_start - 1)
        def _():
            w_copy.wait_recv()

        for step in range(1, half + 1):
            @pl.when(t == SUB * (2 * step - 1) + c_start - 1)
            def _(step=step):
                source = ring(-s * step)
                u_arrived(2 * source + c)
                if step < half:
                    e_copy_long(step + 1).start()
                e_copy_sib(source).start()

        for step in range(1, half):
            @pl.when(t == 2 * SUB * step + c_start - 1)
            def _(step=step):
                source = ring(s * step)
                u_arrived(2 * source + c)
                if step < half - 1:
                    e_copy_short(step + 1).start()
                e_copy_sib(source).start()

        jn = jc + 1

        @pl.when(jnp.logical_and(jnp.logical_and(jn >= 0, jn < pieces),
                                 lax.rem(jn + slots * SUB, SUB) == 0))
        def _():
            q = c_chip(lax.div(jn, SUB))

            @pl.loop(0, feats // TILE)
            def _(tile):
                cut = pl.ds(pl.multiple_of(tile * TILE, TILE), TILE)
                pi[q, :, cut] = lax.dot_general(
                    u[u_rows(2 * q + c), :], w[cut, :], (((1,), (1,)), ((), ())),
                    preferred_element_type=jnp.float32).astype(jnp.bfloat16)

        @pl.when(here)
        def _():
            @pl.when(jnp.logical_and(i > 0, sub < 2))
            def _():
                done = x_chip(i - 1)
                for tile in range(SUB // 2):
                    out_tile(done, sub * (SUB // 2) + tile)

            @pl.when(jnp.logical_and(i > 0, sub == 2))
            def _():
                rotate_own(x_chip(i - 1))

            @pl.when(j == pieces - 1)
            def _():
                q = x_chip(n - 1)

                @pl.loop(0, SUB)
                def _(tile):
                    out_tile(q, tile)

        @pl.when(t == n - 1 + SUB + 3)
        def _():
            rotate_other(p)

            @pl.loop(0, tiles)
            def _(tile):
                at = grad_cols(tile)
                g[:, at] = grad_part(p, at)

        @pl.when(t == n - 1 + SUB * (n - 1) + 2)
        def _():
            across = ring(half)
            rotate_other(across)

            @pl.loop(0, tiles)
            def _(tile):
                at = grad_cols(tile)
                g[:, at] += grad_part(across, at)

        for k in range(half, 0, -1):
            i = 1 if k == half else 2 * (half - k)

            @pl.when(t == n - 1 + SUB * i + SUB + 1)
            def _(k=k):
                if k < half:
                    rl_copy(k + 1).wait_recv()
                    q = ring(s * k)
                    po[q] = add_into(po[q], rs_long[k])
                rl_copy(k).start()

        for k in range(half - 1, 0, -1):
            @pl.when(t == n - 1 + SUB * (2 * (half - k) + 1) + SUB - 1 + 2 * min(k - 1, 1))
            def _(k=k):
                if k < half - 1:
                    rr_copy(k + 1).wait_recv()
                    q = ring(-s * k)
                    po[q] = add_into(po[q], rs_short[k])
                rr_copy(k).start()

    rotate_own(x_chip(n - 1))
    others = [ring(way * k) for k in range(1, half) for way in (1, -1)]
    for q in others:
        rotate_other(q)

    def g_copy(tile):
        at = grad_cols(tile)
        return pltpu.make_async_copy(g.at[:, at], grad_ref.at[:, at], g_sem.at[tile])

    @pl.loop(0, tiles)
    def _(tile):
        at = grad_cols(tile)
        total = g[:, at]
        for q in others:
            total += grad_part(q, at)
        g[:, at] = total
        g_copy(tile).start()

    rl_copy(1).wait_recv()
    rr_copy(1).wait_recv()
    out_ref[...] = (po[p].astype(jnp.float32) + rs_long[0].astype(jnp.float32)
                    + rs_short[0].astype(jnp.float32)).astype(jnp.bfloat16)

    @pl.when(home == 0)
    def _():
        for sub in range(SUB):
            pltpu.make_async_copy(ig_ref.at[part(sub)], ig_ref.at[part(sub)], f_recv.at[sub]).wait()
        d1.wait_send()

    for tile in range(tiles):
        g_copy(tile).wait()
    w_copy.wait_send()
    for step in range(1, half + 1):
        e_copy_long(step).wait_send()
        rl_copy(step).wait_send()
    for step in range(1, half):
        e_copy_short(step).wait_send()
        rr_copy(step).wait_send()

    @pl.loop(0, n)
    def _(q):
        e_copy_sib(q).wait_send()
        xo_copy(q).wait_send()

        @pl.loop(0, SUB)
        def _(sub):
            @pl.when(goes_up)
            def _():
                x_copy(q, sub, 0, z + 1).wait_send()

            @pl.when(goes_down)
            def _():
                x_copy(q, sub, 1, z - 1).wait_send()

            @pl.when(z < p)
            def _():
                c_copy_up(q, sub).wait_send()

            @pl.when(z > p)
            def _():
                c_copy_down(q, sub).wait_send()

            @pl.when(jnp.logical_and(home == 1, q != p))
            def _():
                f_copy(q, sub).wait_send()


COPY_PARTS = 8


def copy_kernel(out_ref, ig_ref, grad_ref, out_to, ig_to, grad_to,
                out_buf, ig_buf, grad_buf, load_sems, store_sems):
    rows = grad_ref.shape[0] // COPY_PARTS
    moves = [(out_ref, out_buf, out_to), (ig_ref, ig_buf, ig_to)]
    for part in range(COPY_PARTS):
        at = pl.ds(part * rows, rows)
        moves.append((grad_ref.at[at], grad_buf.at[at], grad_to.at[at]))
    loads = [pltpu.make_async_copy(source, held, load_sems.at[k])
             for k, (source, held, target) in enumerate(moves)]
    stores = [pltpu.make_async_copy(held, target, store_sems.at[k])
              for k, (source, held, target) in enumerate(moves)]
    for load in loads:
        load.start()
    for load, store in zip(loads, stores):
        load.wait()
        store.start()
    for store in stores:
        store.wait()


def hand_on(arrays):
    hbm = pl.BlockSpec(memory_space=pl.ANY)
    return pl.pallas_call(
        copy_kernel,
        out_shape=tuple(jax.ShapeDtypeStruct(a.shape, a.dtype) for a in arrays),
        in_specs=[hbm] * 3,
        out_specs=(hbm,) * 3,
        scratch_shapes=[pltpu.VMEM(a.shape, a.dtype) for a in arrays]
        + [pltpu.SemaphoreType.DMA((2 + COPY_PARTS,))] * 2,
        compiler_params=pltpu.CompilerParams(vmem_limit_bytes=60 << 20),
    )(*arrays)


def fused(acts, w_rot, signs, upstream):
    n = lax.axis_size("node")
    tok, feats = acts.shape
    rows, cols = w_rot.shape
    blocks = rows // HBLK
    half = n // 2
    had = sylvester(HBLK)
    own_signs = lax.dynamic_slice_in_dim(signs, lax.axis_index("local") * rows, rows)
    own_signs = own_signs.astype(jnp.float32).reshape(blocks, HBLK)
    left = (own_signs[:, :, None] * had).astype(jnp.bfloat16)
    right = (own_signs[:, None, :] * had).astype(jnp.bfloat16)
    bf = jnp.bfloat16
    dma = pltpu.SemaphoreType.DMA
    vmem = pl.BlockSpec(memory_space=pltpu.VMEM)
    hbm = pl.BlockSpec(memory_space=pl.ANY)
    tokens = 2 * n * tok
    return hand_on(pl.pallas_call(
        functools.partial(kernel, n),
        out_shape=(
            jax.ShapeDtypeStruct((tok, cols), bf),
            jax.ShapeDtypeStruct((tok, feats), bf),
            jax.ShapeDtypeStruct((rows, cols), jnp.float32),
        ),
        in_specs=[hbm, hbm, hbm, vmem, vmem],
        out_specs=(vmem, vmem, hbm),
        scratch_shapes=[
            pltpu.VMEM((feats, cols), bf),
            pltpu.VMEM((n, tok, feats), bf),
            pltpu.VMEM((n, tok, rows), bf),
            pltpu.VMEM((rows, tokens), bf),
            pltpu.VMEM((tokens, cols), bf),
            pltpu.VMEM((n, tok, feats), bf),
            pltpu.VMEM((n, tok, feats), bf),
            pltpu.VMEM((n, tok, feats), bf),
            pltpu.VMEM((n, tok, cols), bf),
            pltpu.VMEM((half, tok, cols), bf),
            pltpu.VMEM((half - 1, tok, cols), bf),
            pltpu.VMEM((rows, cols), jnp.float32),
            dma((2 + rows // tok,)), dma, dma((n,)), dma((2, n * SUB)), dma((n * SUB,)), dma((n,)), dma((n,)),
            dma((half,)), dma((half - 1,)), dma((n,)), dma((2 * n,)), dma((2,)),
            dma((n * SUB,)), dma((2, n * SUB)), dma((n * SUB,)), dma((SUB,)),
            dma((half,)), dma((half,)), dma((half - 1,)), dma((half - 1,)), dma((cols // GRAD_TILE,)),
        ],
        compiler_params=pltpu.CompilerParams(
            collective_id=0, has_side_effects=True, vmem_limit_bytes=60 << 20),
        cost_estimate=pl.CostEstimate(
            flops=6 * tokens * rows * cols, bytes_accessed=16 * rows * cols, transcendentals=0),
    )(acts, w_rot, upstream, left, right))


def solution(mesh):
    spec = P("local", "node")
    n = mesh.shape["node"]
    paired = mesh.shape["local"] == 2 * n and n >= 4 and n % 2 == 0
    return jax.shard_map(
        fused if paired else local, mesh=mesh, in_specs=(spec, spec, P(), spec),
        out_specs=(spec, spec, spec), check_vma=False,
    )
```
